32 devices in a mesh: hid: 4 (over x, core), ep: 8 (over z, y).
Axes of the slice: x: 2, y: 2, z: 4, core: 2. Of those that a mesh axis runs over, the one named last changes fastest.
Arguments:
- gate_proj: bfloat16 [2, 7168, 2048], P(None, 'hid', 'ep'), may hold values from -6 to 6
- up_proj: bfloat16 [2, 7168, 2048], P(None, 'hid', 'ep'), may hold values from -6 to 6
- down_proj: bfloat16 [2, 2048, 7168], P(None, 'ep', 'hid'), may hold values from -6 to 6
- rotation: bfloat16 [7168, 7168], P('hid'), may hold values from -0.0625 to 0.0625
- placement: int32 [2, 8], replicated, may hold values from 0 to 7, each once within a row
- row_count: int32 [2, 8], replicated, may hold values from 64 to 512, as said below
Outputs:
- served: bfloat16 [8, 1024, 3, 7168], P('ep', 'hid')
The draws below stay inside these ranges and needn't reach their ends.
Inputs may be any that keep to these rules, and one draw needn't show every extreme that they name: `row_count`: every count is a multiple of 64, each expert's counts sum to 2048, and one owner holds 512 rows of every expert.
All inputs are finite; a program needn't handle non-finite values.
Results may differ from the reference program's by a relative error of at most 0.017.
Values may be sent and summed in bfloat16 or wider, within the bound.
No kernel may reach another device: no remote copies, remote signals or barrier semaphores. Data moves between devices by JAX's collectives and lax.ppermute only.
A program may use at most 192 MiB of HBM per device.

```python
import jax
import jax.numpy as jnp

H = 7168
F = 2048
EXP = 2
OWNERS = 8
HID_SHARDS = 4
BLOCKS = 32
SUB = 64
SLOTS_DEV = 256
SLOTS = 1024
N_HID = 4


def draw_row_count(key, part):
    key = jax.random.fold_in(key, 7)
    key_busiest, key_spread = jax.random.split(key)
    busiest = jax.random.randint(key_busiest, (), 0, OWNERS)
    spare_room = 2 * HID_SHARDS - 1
    extra_total = BLOCKS - 2 * HID_SHARDS - (OWNERS - 1)
    tokens = jnp.repeat(jnp.arange(OWNERS - 1, dtype=jnp.int32), spare_room)

    def one_expert(sub_key):
        shuffled = jax.random.permutation(sub_key, tokens)
        taken_ids = shuffled[:extra_total]
        extra_blocks = jnp.sum((taken_ids[:, None] == jnp.arange(OWNERS - 1, dtype=jnp.int32)[None, :]).astype(jnp.int32), axis=0)
        others = 1 + extra_blocks
        owner_ids = jnp.arange(OWNERS, dtype=jnp.int32)
        other_index = jnp.clip(owner_ids - (owner_ids > busiest).astype(jnp.int32), 0, OWNERS - 2)
        return jnp.where(owner_ids == busiest, 2 * HID_SHARDS, others[other_index]) * SUB
    return jax.vmap(one_expert)(jax.random.split(key_spread, EXP)).astype(jnp.int32)


def level_of(key, extent, cuts, low, largest):
    factor_of, own = 1.0, jax.random.fold_in(key, 6)
    for dim, parts in cuts:
        draws = jnp.exp(jax.random.uniform(jax.random.fold_in(own, dim), (parts,), jnp.float32, low / len(cuts), largest / len(cuts)))
        factor_of = factor_of * jnp.repeat(draws, extent[dim] // parts).reshape([-1 if axis == dim else 1 for axis in range(len(extent))])
    return factor_of


def scatter_about(own_key, dims, deviation, most, cuts=(), held_as=jnp.bfloat16):
    values = jax.random.normal(own_key, dims, jnp.float32) * deviation
    if len(cuts) > 0:
        values = level_of(own_key, dims, cuts, -0.22, 0.18) * values
    return jnp.clip(values, min=-most, max=most).astype(held_as)


def setup_inputs(seed: int = 0) -> dict:
    seeds = jax.random.split(jax.random.key(seed), 7)
    return {
        "gate_proj": scatter_about(seeds[0], (EXP, H, F), 1.0, 6.0, ((1, 4), (2, 8))),
        "up_proj": scatter_about(seeds[1], (EXP, H, F), 1.0, 6.0, ((1, 4), (2, 8))),
        "down_proj": scatter_about(seeds[2], (EXP, F, H), 1.0, 6.0, ((1, 8), (2, 4))),
        "rotation": scatter_about(seeds[3], (H, H), H ** -0.5, 0.0625, ((0, 4),)),
        "placement": jax.vmap(lambda own: jax.random.permutation(own, OWNERS))(jax.random.split(seeds[4], EXP)).reshape((EXP, OWNERS)).astype(jnp.int32),
        "row_count": draw_row_count(jax.random.fold_in(seeds[6], 71), 0),
    }


def count_below(bound, residue, shard_total):
    return ((bound + shard_total - 1 - residue) // shard_total).astype(jnp.int32)


def routing(placement, row_count, block_rows):
    owner_total = placement.shape[1]
    blocks = (row_count // block_rows).astype(jnp.int32)
    onehot = (placement[:, :, None] == jnp.arange(owner_total, dtype=jnp.int32)[None, None, :]).astype(jnp.int32)
    ordered = jnp.sum(onehot * blocks[:, None, :], axis=2).astype(jnp.int32)
    ordered_start = (jnp.cumsum(ordered, axis=1) - ordered).astype(jnp.int32)
    first_block = jnp.sum(onehot * ordered_start[:, :, None], axis=1).astype(jnp.int32)
    return blocks, first_block


def reference(gate_proj, up_proj, down_proj, rotation, placement, row_count):
    sources = [jnp.transpose(gate_proj, (0, 2, 1)), jnp.transpose(up_proj, (0, 2, 1)), down_proj]
    piece_width = H // N_HID
    results = []
    for expert in range(EXP):
        per_kind = []
        for source in sources:
            accumulated = jnp.zeros((F, H), jnp.float32)
            for hid_block in range(N_HID):
                columns = source[expert][:, hid_block * piece_width:(hid_block + 1) * piece_width]
                term = jnp.dot(columns, rotation[hid_block * piece_width:(hid_block + 1) * piece_width], preferred_element_type=jnp.float32)
                accumulated = accumulated + term.astype(jnp.bfloat16).astype(jnp.float32)
            per_kind.append(accumulated.astype(jnp.bfloat16))
        results.append(jnp.stack(per_kind, axis=1))
    rotated = jnp.stack(results)
    blocks, first_block = routing(placement, row_count, SUB)
    block_ids = jnp.arange(BLOCKS, dtype=jnp.int32)
    residue = (block_ids % N_HID).astype(jnp.int32)
    inside = ((first_block[:, None, :] <= block_ids[None, :, None]) & (block_ids[None, :, None] < (first_block + blocks)[:, None, :])).astype(jnp.int32)
    owner_ids = jnp.arange(OWNERS, dtype=jnp.int32)
    target_owner = jnp.sum(inside * owner_ids[None, None, :], axis=2).astype(jnp.int32)
    shard_ids = jnp.arange(N_HID, dtype=jnp.int32)
    at_shard = count_below((first_block + blocks)[:, :, None], shard_ids[None, None, :], N_HID) - count_below(first_block[:, :, None], shard_ids[None, None, :], N_HID)
    offset = (jnp.cumsum(at_shard, axis=0) - at_shard).astype(jnp.int32)
    offset_here = jnp.transpose(jnp.take(offset, residue, axis=2), (0, 2, 1))
    base_here = count_below(first_block[:, None, :], residue[None, :, None], N_HID)
    slot_index = jnp.sum(inside * (offset_here - base_here), axis=2).astype(jnp.int32) + count_below(block_ids, residue, N_HID)[None, :]
    position = residue[None, :] * SLOTS_DEV + slot_index * SUB
    row_ids = position[:, :, None] + jnp.arange(SUB, dtype=jnp.int32)[None, None, :]
    owner_rows = jnp.broadcast_to(target_owner[:, :, None], row_ids.shape)
    values = rotated.reshape(EXP * F, 3, H)
    served = jnp.zeros((OWNERS, SLOTS, 3, H), jnp.bfloat16)
    served = served.at[owner_rows.reshape(-1), row_ids.reshape(-1)].set(values)
    return served
```

```python
import functools

import jax
import jax.numpy as jnp
from jax import lax
from jax.experimental import pallas as pl
from jax.experimental.pallas import tpu as pltpu
from jax.sharding import PartitionSpec as P

CHUNK_TILES = (1, 1, 2, 2, 2, 2, 2, 1, 1)
MATMUL_VMEM = 16 * 2**20
MOVE_VMEM = 8 * 2**20
COST = pl.CostEstimate(flops=20000000000, bytes_accessed=2**10, transcendentals=0)
ORDER = (
    'S0',
    'S1',
    'S2',
    'K0',
    'K1',
    'K2',
    'A0',
    'S3',
    'A1',
    'I0',
    'K3',
    'I1',
    'M0',
    'A2',
    'S4',
    'M1',
    'I2',
    'K4',
    'O0',
    'A3',
    'M2',
    'I3',
    'O1',
    'A4',
    'P0',
    'I4',
    'M3',
    'P1',
    'L0',
    'S5',
    'O2',
    'L1',
    'K5',
    'S6',
    'M4',
    'K6',
    'A5',
    'O3',
    'P2',
    'I5',
    'A6',
    'L2',
    'S7',
    'M5',
    'I6',
    'O4',
    'K7',
    'P3',
    'A7',
    'M6',
    'L3',
    'S8',
    'I7',
    'O5',
    'K8',
    'P4',
    'M7',
    'A8',
    'L4',
    'O6',
    'I8',
    'P5',
    'M8',
    'O7',
    'L5',
    'O8',
    'P6',
    'P7',
    'L6',
    'L7',
    'P8',
    'L8',
)
MARK = jax.ShapeDtypeStruct((8, 128), jnp.float32)
KINDS = 3
SLOT_TOTAL = 4
ROWS_Z = 4
LINK_CAP = 8
AT_MID, AT_OUT, AT_PARTNER, AT_OWN, TABLE = 0, 8, 16, 20, 32
KEEP, SIDE, FAR_KEEP, FAR_SIDE, MID, OUT, CODES = 0, 2, 4, 6, 8, 16, 24
NEAR_CODES, FAR_CODES, MID_CODES, OUT_CODES = (0, 4), (4, 8), (8, 16), (16, 24)


def route_kernel(here_ref, placement_ref, row_count_ref, table_ref, *, owners, hid_total, block_rows):
    hid, ep = here_ref[0], here_ref[1]
    z, y = ep // 2, ep % 2
    experts = placement_ref.shape[0]
    pieces = [(e, s) for e in range(experts) for s in range(owners)]
    owner = {}
    for e in range(experts):
        start = jnp.int32(0)
        found = [jnp.int32(0)] * owners
        for j in range(owners):
            o = placement_ref[e, j]
            stop = start + row_count_ref[e, o] // block_rows
            for s in range(owners):
                q = s * hid_total + hid
                found[s] = jnp.where((start <= q) & (q < stop), o, found[s])
            start = stop
        for s in range(owners):
            owner[e, s] = found[s]
    upper = z >= 2
    mid_row = (z == 1) | (z == 2)

    def half(row):
        return row >= 2

    zero = jnp.int32(0)
    mid_in, mid_out, out_in, out_out = zero, zero, zero, zero
    for i in range(TABLE):
        table_ref[i] = jnp.int32(-1)
    mine, partner = zero, zero
    for e, s in pieces:
        row, side = s // 2, s % 2
        o = owner[e, s]
        drow = o // 2
        goes_up, goes_down = drow >= 2, drow < 2
        crosses = goes_up if row < 2 else goes_down
        from_here_half = jnp.logical_not(upper) if row < 2 else upper
        leaves_mid = crosses & from_here_half
        enters_mid = crosses & jnp.logical_not(from_here_half)
        to_top = (drow == ROWS_Z - 1) if row < ROWS_Z - 1 else jnp.bool_(False)
        to_bottom = (drow == 0) if row > 0 else jnp.bool_(False)
        on_outer = jnp.where(upper, to_top, to_bottom)
        near_far = z == row
        outer_row = jnp.where(upper, ROWS_Z - 1, 0)
        from_outer = mid_row & (outer_row == row)
        code = jnp.where(
            near_far,
            jnp.where(y == side, KEEP + e, SIDE + e),
            jnp.where(
                from_outer,
                jnp.where(y == side, FAR_KEEP + e, FAR_SIDE + e),
                jnp.where(mid_row, MID + mid_in, OUT + out_in),
            ),
        )

        @pl.when(leaves_mid & mid_row)
        def _(mid_out=mid_out, code=code):
            table_ref[AT_MID + mid_out] = code

        @pl.when(on_outer & mid_row)
        def _(out_in=out_in, code=code):
            table_ref[AT_OUT + out_in] = code

        is_mine = o == ep
        is_partner = (drow == z) & (o != ep)

        @pl.when(is_mine)
        def _(mine=mine, code=code):
            table_ref[AT_OWN + mine] = code

        @pl.when(is_partner)
        def _(partner=partner, code=code):
            table_ref[AT_PARTNER + partner] = code

        mid_out = mid_out + leaves_mid.astype(jnp.int32)
        mid_in = mid_in + enters_mid.astype(jnp.int32)
        out_in = out_in + on_outer.astype(jnp.int32)
        mine = mine + is_mine.astype(jnp.int32)
        partner = partner + is_partner.astype(jnp.int32)


def route(here, placement, row_count, hid_total, block_rows):
    smem = pl.BlockSpec(memory_space=pltpu.SMEM)
    return pl.pallas_call(
        functools.partial(
            route_kernel,
            owners=placement.shape[1],
            hid_total=hid_total,
            block_rows=block_rows,
        ),
        out_shape=jax.ShapeDtypeStruct((TABLE,), jnp.int32),
        in_specs=[smem] * 3,
        out_specs=smem,
        compiler_params=pltpu.CompilerParams(vmem_limit_bytes=MOVE_VMEM),
        name="route",
    )(here, placement, row_count)


ANYWHERE = pl.BlockSpec(memory_space=pl.ANY)
ON_SMEM = pl.BlockSpec(memory_space=pltpu.SMEM)
ON_VMEM = pl.BlockSpec(memory_space=pltpu.VMEM)
TILE = 512


def gather_rows_kernel(gate_ref, up_ref, down_ref, out_ref):
    rows = out_ref.shape[4]
    for kind, ref in enumerate((gate_ref, up_ref, down_ref)):
        block = ref[0] if kind == 2 else ref[0].T
        for x in range(2):
            for core in range(2):
                first = (2 * x + core) * rows
                out_ref[core, x, 0, kind] = block[first : first + rows]


def gather_rows(gate_proj, up_proj, down_proj):
    experts, depth, local_rows = gate_proj.shape
    block_rows = local_rows // 4
    across = pl.BlockSpec((1, depth, local_rows), lambda e: (e, 0, 0))
    along = pl.BlockSpec((1, local_rows, depth), lambda e: (e, 0, 0))
    rows = pl.pallas_call(
        gather_rows_kernel,
        out_shape=jax.ShapeDtypeStruct((2, 2, experts, KINDS, block_rows, depth), jnp.bfloat16),
        grid=(experts,),
        in_specs=[across, across, along],
        out_specs=pl.BlockSpec(
            (2, 2, 1, KINDS, block_rows, depth), lambda e: (0, 0, e, 0, 0, 0)
        ),
        compiler_params=pltpu.CompilerParams(vmem_limit_bytes=32 * 2**20),
        name="gather_rows",
    )(gate_proj, up_proj, down_proj)
    return rows.reshape(2, 2 * experts * KINDS * block_rows, depth)


def product(lhs_ref, top_ref, bottom_ref):
    depth = top_ref.shape[0]
    return jnp.dot(
        lhs_ref[0, :, :depth], top_ref[...], preferred_element_type=jnp.float32
    ) + jnp.dot(lhs_ref[0, :, depth:], bottom_ref[...], preferred_element_type=jnp.float32)


def send_kernel(here_ref, lhs_ref, top_ref, bottom_ref, after_ref, out_ref, mark_ref):
    out_ref[...] = product(lhs_ref, top_ref, bottom_ref).astype(jnp.bfloat16)


def keep_kernel(
    here_ref, lhs_ref, top_ref, bottom_ref, recv_ref, after_ref, away_ref, home_ref, mark_ref
):
    rows = away_ref.shape[0]
    total = product(lhs_ref, top_ref, bottom_ref) + recv_ref[...].astype(jnp.float32)
    total = total.astype(jnp.bfloat16)
    x = here_ref[0] // 2

    @pl.when(x == 0)
    def _():
        home_ref[...] = total[:rows]
        away_ref[...] = total[rows:]

    @pl.when(x == 1)
    def _():
        home_ref[...] = total[rows:]
        away_ref[...] = total[:rows]


def matmul_specs(lhs, column, send):
    _, rows, depth = lhs.shape

    def lhs_map(tile, here):
        core = here[0] % 2
        return (1 - core if send else core, 0, 0)

    def rot_map(part, tile, here):
        return (part, column // TILE + tile)

    return [
        pl.BlockSpec((1, rows, depth), lhs_map, pipeline_mode=pl.Buffered(1)),
        pl.BlockSpec((depth // 2, TILE), functools.partial(rot_map, 0)),
        pl.BlockSpec((depth // 2, TILE), functools.partial(rot_map, 1)),
    ]


def matmul_send(here, lhs, rotation, column, width, after, cost):
    _, rows, _ = lhs.shape
    return pl.pallas_call(
        send_kernel,
        out_shape=(jax.ShapeDtypeStruct((rows, width), jnp.bfloat16), MARK),
        grid_spec=pltpu.PrefetchScalarGridSpec(
            num_scalar_prefetch=1,
            grid=(width // TILE,),
            in_specs=matmul_specs(lhs, column, True) + [ANYWHERE],
            out_specs=(pl.BlockSpec((rows, TILE), lambda t, here: (0, t)), ANYWHERE),
        ),
        compiler_params=pltpu.CompilerParams(vmem_limit_bytes=MATMUL_VMEM),
        cost_estimate=cost,
        name="matmul_send",
    )(here, lhs, rotation, rotation, after)


def matmul_keep(here, lhs, rotation, recv, column, width, after, cost):
    _, rows, _ = lhs.shape
    out = jax.ShapeDtypeStruct((rows // 2, width), jnp.bfloat16)
    out_spec = pl.BlockSpec((rows // 2, TILE), lambda t, here: (0, t))
    recv_spec = pl.BlockSpec((rows, TILE), lambda t, here: (0, t))
    return pl.pallas_call(
        keep_kernel,
        out_shape=(out, out, MARK),
        grid_spec=pltpu.PrefetchScalarGridSpec(
            num_scalar_prefetch=1,
            grid=(width // TILE,),
            in_specs=matmul_specs(lhs, column, False) + [recv_spec, ANYWHERE],
            out_specs=(out_spec, out_spec, ANYWHERE),
        ),
        compiler_params=pltpu.CompilerParams(vmem_limit_bytes=MATMUL_VMEM),
        cost_estimate=cost,
        name="matmul_keep",
    )(here, lhs, rotation, rotation, recv, after)


def add_kernel(here_ref, home_ref, recv_ref, after_ref, side_ref, keep_ref, mark_ref):
    width = side_ref.shape[1]
    y = here_ref[1] % 2
    for half, ref in ((1 - y, side_ref), (y, keep_ref)):
        part = pl.ds(pl.multiple_of(half * width, 128), width)
        total = home_ref[:, part].astype(jnp.float32) + recv_ref[:, part].astype(jnp.float32)
        ref[...] = total.astype(jnp.bfloat16)


def add(here, home, recv, after, cost):
    rows, width = home.shape
    tile = 128
    out = jax.ShapeDtypeStruct((rows, width // 2), jnp.bfloat16)
    in_spec = pl.BlockSpec((tile, width), lambda i, here: (i, 0))
    out_spec = pl.BlockSpec((tile, width // 2), lambda i, here: (i, 0))
    return pl.pallas_call(
        add_kernel,
        out_shape=(out, out, MARK),
        grid_spec=pltpu.PrefetchScalarGridSpec(
            num_scalar_prefetch=1,
            grid=(rows // tile,),
            in_specs=[in_spec, in_spec, ANYWHERE],
            out_specs=(out_spec, out_spec, ANYWHERE),
        ),
        compiler_params=pltpu.CompilerParams(vmem_limit_bytes=MOVE_VMEM),
        cost_estimate=cost,
        name="add",
    )(here, home, recv, after)


def start_pick(code, bases, sources, target, sem):
    for source, (low, high) in zip(sources, bases):

        @pl.when((code >= low) & (code < high))
        def _(source=source, low=low):
            pltpu.make_async_copy(source.at[code - low], target, sem).start()


def pick_kernel(table_ref, *refs, first, bases):
    sources, out_ref, sems = refs[: len(bases)], refs[-3], refs[-1]
    total = out_ref.shape[0]
    for i in range(total):
        start_pick(table_ref[first + i], bases, sources, out_ref.at[i], sems.at[i])
    for i in range(total):

        @pl.when(table_ref[first + i] >= 0)
        def _(i=i):
            pltpu.make_async_copy(sources[0].at[0], out_ref.at[i], sems.at[i]).wait()


def pick(table, sources, bases, first, total, after, cost):
    piece = sources[0].shape[1:]
    return pl.pallas_call(
        functools.partial(pick_kernel, first=first, bases=bases),
        out_shape=(jax.ShapeDtypeStruct((total,) + piece, jnp.bfloat16), MARK),
        in_specs=[ON_SMEM] + [ANYWHERE] * (len(sources) + 1),
        out_specs=(ON_VMEM, ANYWHERE),
        scratch_shapes=[pltpu.SemaphoreType.DMA((total,))],
        cost_estimate=cost,
        compiler_params=pltpu.CompilerParams(vmem_limit_bytes=MOVE_VMEM),
        name="pick",
    )(table, *sources, after)


def pack_kernel(keep_ref, side_ref, after_ref, out_ref, mark_ref, sems):
    experts = keep_ref.shape[0]
    copies = [
        pltpu.make_async_copy(ref, out_ref.at[pl.ds(n * experts, experts)], sems.at[n])
        for n, ref in enumerate((keep_ref, side_ref))
    ]
    for copy in copies:
        copy.start()
    for copy in copies:
        copy.wait()


def pack(keep, side, after, cost):
    experts = keep.shape[0]
    return pl.pallas_call(
        pack_kernel,
        out_shape=(jax.ShapeDtypeStruct((2 * experts,) + keep.shape[1:], jnp.bfloat16), MARK),
        in_specs=[ANYWHERE] * 3,
        out_specs=(ON_VMEM, ANYWHERE),
        scratch_shapes=[pltpu.SemaphoreType.DMA((2,))],
        compiler_params=pltpu.CompilerParams(vmem_limit_bytes=MOVE_VMEM),
        cost_estimate=cost,
        name="pack",
    )(keep, side, after)


def place_kernel(here_ref, table_ref, *refs, bases, column):
    sources, partner_ref = refs[: len(bases)], refs[len(bases)]
    out_ref, mark_ref, held_ref, in_sems, out_sems = refs[-5:]
    _, _, _, rows, width = held_ref.shape
    y = here_ref[1] % 2

    def target(slot, half):
        at = pl.multiple_of(column + half * width, 128)
        return out_ref.at[:, pl.ds(slot * rows, rows), pl.ds(at, width)]

    for slot in range(SLOT_TOTAL):
        code = table_ref[AT_OWN + slot]
        start_pick(code, bases, sources, held_ref.at[slot, 0], in_sems.at[slot, 0])

        @pl.when(code >= 0)
        def _(slot=slot):
            pltpu.make_async_copy(
                partner_ref.at[slot], held_ref.at[slot, 1], in_sems.at[slot, 1]
            ).start()

        @pl.when(code < 0)
        def _(slot=slot):
            held_ref[slot] = jnp.zeros(held_ref.shape[1:], held_ref.dtype)

    for slot in range(SLOT_TOTAL):

        @pl.when(table_ref[AT_OWN + slot] >= 0)
        def _(slot=slot):
            for part in range(2):
                pltpu.make_async_copy(
                    partner_ref.at[slot], held_ref.at[slot, part], in_sems.at[slot, part]
                ).wait()

        pltpu.make_async_copy(held_ref.at[slot, 0], target(slot, y), out_sems.at[slot, 0]).start()
        pltpu.make_async_copy(
            held_ref.at[slot, 1], target(slot, 1 - y), out_sems.at[slot, 1]
        ).start()
    for slot in range(SLOT_TOTAL):
        pltpu.make_async_copy(held_ref.at[slot, 0], target(slot, y), out_sems.at[slot, 0]).wait()
        pltpu.make_async_copy(
            held_ref.at[slot, 1], target(slot, 1 - y), out_sems.at[slot, 1]
        ).wait()


def place(here, table, sources, bases, partner, column, full_width, previous, after, cost):
    piece = partner.shape[1:]
    operands = [here, table, *sources, partner, after]
    in_specs = [ON_SMEM, ON_SMEM] + [ANYWHERE] * (len(sources) + 2)
    aliases = {}
    if previous is not None:
        aliases = {len(operands): 0}
        operands.append(previous)
        in_specs.append(ANYWHERE)
    return pl.pallas_call(
        functools.partial(place_kernel, bases=bases, column=column),
        out_shape=(
            jax.ShapeDtypeStruct((KINDS, SLOT_TOTAL * piece[1], full_width), jnp.bfloat16),
            MARK,
        ),
        in_specs=in_specs,
        out_specs=(ANYWHERE, ANYWHERE),
        scratch_shapes=[
            pltpu.VMEM((SLOT_TOTAL, 2) + piece, jnp.bfloat16),
            pltpu.SemaphoreType.DMA((SLOT_TOTAL, 2)),
            pltpu.SemaphoreType.DMA((SLOT_TOTAL, 2)),
        ],
        input_output_aliases=aliases,
        cost_estimate=cost,
        compiler_params=pltpu.CompilerParams(vmem_limit_bytes=MOVE_VMEM),
        name="place",
    )(*operands)


def pipelined(gate_proj, up_proj, down_proj, rotation, placement, row_count):
    hid_total = lax.axis_size("hid")
    experts, depth, local_rows = gate_proj.shape
    full_width = rotation.shape[1]
    block_rows = local_rows // hid_total
    here = jnp.stack([lax.axis_index("hid"), lax.axis_index("ep")]).astype(jnp.int32)
    table = route(here, placement, row_count, hid_total, block_rows)

    lhs = gather_rows(gate_proj, up_proj, down_proj)

    cores = [(h, h ^ 1) for h in range(4)]
    along_x = [(h, h ^ 2) for h in range(4)]
    along_y = [(s, s ^ 1) for s in range(8)]
    inward = [(0, 2), (1, 3), (6, 4), (7, 5)]
    middle = [(2, 4), (3, 5), (4, 2), (5, 3)]
    outward = [(4, 6), (5, 7), (2, 0), (3, 1)]
    widths = [tiles * TILE for tiles in CHUNK_TILES]
    columns = [sum(widths[:i]) for i in range(len(widths))]
    chunks = len(widths)

    core_recv, x_recv, home, keep, side = {}, {}, {}, {}, {}
    near, far, mid, outer, partner = {}, {}, {}, {}, {}
    all_codes = [NEAR_CODES, FAR_CODES, MID_CODES, OUT_CODES]

    def send_terms(i, served, *order):
        sent, mark = matmul_send(here, lhs, rotation, columns[i], widths[i], *order)
        core_recv[i] = lax.ppermute(sent, "hid", cores)
        return served, mark

    def keep_terms(i, served, *order):
        recv = core_recv.pop(i)
        away, home[i], mark = matmul_keep(here, lhs, rotation, recv, columns[i], widths[i], *order)
        x_recv[i] = lax.ppermute(away, "hid", along_x)
        return served, mark

    def sum_terms(i, served, *order):
        pieces = (experts, KINDS, block_rows, widths[i] // 2)
        out, own, mark = add(here, home.pop(i), x_recv.pop(i), *order)
        keep[i] = own.reshape(pieces)
        side[i] = lax.ppermute(out.reshape(pieces), "ep", along_y)
        return served, mark

    def send_inward(i, served, *order):
        near[i], mark = pack(keep.pop(i), side.pop(i), *order)
        far[i] = lax.ppermute(near[i], "ep", inward)
        return served, mark

    def send_across(i, served, *order):
        codes = [NEAR_CODES, FAR_CODES]
        out, mark = pick(table, [near[i], far[i]], codes, AT_MID, LINK_CAP, *order)
        mid[i] = lax.ppermute(out, "ep", middle)
        return served, mark

    def send_outward(i, served, *order):
        codes = [NEAR_CODES, MID_CODES]
        out, mark = pick(table, [near[i], mid[i]], codes, AT_OUT, LINK_CAP, *order)
        outer[i] = lax.ppermute(out, "ep", outward)
        return served, mark

    def send_partner(i, served, *order):
        sources = [near[i], far[i], mid[i], outer[i]]
        out, mark = pick(table, sources, all_codes, AT_PARTNER, SLOT_TOTAL, *order)
        partner[i] = lax.ppermute(out, "ep", along_y)
        return served, mark

    def put(i, served, *order):
        sources = [near.pop(i), far.pop(i), mid.pop(i), outer.pop(i)]
        return place(
            here, table, sources, all_codes, partner.pop(i), columns[i], full_width, served, *order
        )

    stages = dict(
        S=send_terms,
        K=keep_terms,
        A=sum_terms,
        I=send_inward,
        M=send_across,
        O=send_outward,
        P=send_partner,
        L=put,
    )
    served, mark = None, here
    for step in ORDER:
        served, mark = stages[step[0]](int(step[1:]), served, mark, COST)
    return served.transpose(1, 0, 2)[None]


def count_below(bound, residue, shard_total):
    return (bound + shard_total - 1 - residue) // shard_total


def routing(placement, row_count, block_rows):
    owner_total = placement.shape[1]
    blocks = row_count // block_rows
    onehot = (
        placement[:, :, None] == jnp.arange(owner_total, dtype=jnp.int32)[None, None, :]
    ).astype(jnp.int32)
    ordered = jnp.sum(onehot * blocks[:, None, :], axis=2)
    ordered_start = jnp.cumsum(ordered, axis=1) - ordered
    first_block = jnp.sum(onehot * ordered_start[:, :, None], axis=1)
    return (blocks, first_block)


def assemble(received, received_slot, slot_blocks, experts):
    flat_slot = received_slot.reshape(-1)
    matches = flat_slot[None, :] == jnp.arange(slot_blocks, dtype=jnp.int32)[:, None]
    present = jnp.any(matches, axis=1)
    picked = jnp.argmax(matches, axis=1)
    source_ids = picked // experts
    expert_ids = picked % experts
    chosen = received[source_ids, :, expert_ids]
    chosen = jnp.where(present[:, None, None, None], chosen, jnp.zeros((), jnp.bfloat16))
    return chosen.reshape(1, slot_blocks * chosen.shape[1], chosen.shape[2], chosen.shape[3])


def gathered(gate_proj, up_proj, down_proj, rotation, placement, row_count):
    shard_total = lax.axis_size("hid")
    owner_total = lax.axis_size("ep")
    experts, width_part, local_rows = gate_proj.shape
    full_width = rotation.shape[1]
    block_rows = local_rows // shard_total
    stacked = jnp.stack(
        [
            jnp.transpose(gate_proj, (2, 0, 1)),
            jnp.transpose(up_proj, (2, 0, 1)),
            jnp.transpose(down_proj, (1, 0, 2)),
        ],
        axis=2,
    )
    stacked = stacked.reshape(local_rows, experts * 3, width_part)
    summed = lax.psum_scatter(
        jnp.einsum("fck,kh->fch", stacked, rotation, preferred_element_type=jnp.float32).astype(
            jnp.bfloat16
        ),
        "hid",
        scatter_dimension=0,
        tiled=True,
    )
    rotated = summed.reshape(block_rows, experts, 3, full_width)
    shard_here = lax.axis_index("hid")
    owner_here = lax.axis_index("ep")
    block_here = owner_here * shard_total + shard_here
    blocks, first_block = routing(placement, row_count, block_rows)
    inside = ((first_block <= block_here) & (block_here < first_block + blocks)).astype(jnp.int32)
    owner_ids = jnp.arange(owner_total, dtype=jnp.int32)
    target_owner = jnp.sum(inside * owner_ids[None, :], axis=1)
    at_shard = count_below(first_block + blocks, shard_here, shard_total) - count_below(
        first_block, shard_here, shard_total
    )
    offset = jnp.cumsum(at_shard, axis=0) - at_shard
    slot_index = jnp.sum(
        inside * (offset - count_below(first_block, shard_here, shard_total)), axis=1
    )
    slot_index = slot_index + count_below(block_here, shard_here, shard_total)
    slot_blocks = 2 * experts
    all_blocks, all_owner, all_slot = (
        lax.all_gather(rotated[None], "ep", axis=0, tiled=True),
        lax.all_gather(target_owner[None], "ep", axis=0, tiled=True),
        lax.all_gather(slot_index[None], "ep", axis=0, tiled=True),
    )
    received_slot = jnp.where(all_owner == owner_here, all_slot, -1)
    return assemble(all_blocks, received_slot, slot_blocks, experts)


def solution(mesh):
    in_specs = (
        P(None, "hid", "ep"),
        P(None, "hid", "ep"),
        P(None, "ep", "hid"),
        P("hid", None),
        P(),
        P(),
    )
    out_specs = P("ep", "hid", None, None)
    fits = mesh.shape["hid"] == 4 and mesh.shape["ep"] == 8
    return jax.shard_map(
        pipelined if fits else gathered,
        mesh=mesh,
        in_specs=in_specs,
        out_specs=out_specs,
        check_vma=False,
    )
```

```python
import functools

import jax
import jax.numpy as jnp
from jax import lax
from jax.experimental import pallas as pl
from jax.experimental.pallas import tpu as pltpu
from jax.sharding import PartitionSpec as P

CHUNK_TILES = (1, 1, 2, 2, 2, 2, 2, 1, 1)
MATMUL_VMEM = 16 * 2**20
MOVE_VMEM = 8 * 2**20
COST = pl.CostEstimate(flops=25000000000, bytes_accessed=2**10, transcendentals=0)
ORDER = (
    'S0',
    'K0',
    'S1',
    'S2',
    'K1',
    'K2',
    'A0',
    'S3',
    'A1',
    'I0',
    'K3',
    'I1',
    'M0',
    'A2',
    'S4',
    'M1',
    'I2',
    'K4',
    'O0',
    'A3',
    'M2',
    'I3',
    'O1',
    'A4',
    'P0',
    'I4',
    'M3',
    'P1',
    'L0',
    'S5',
    'O2',
    'L1',
    'K5',
    'S6',
    'M4',
    'K6',
    'A5',
    'O3',
    'P2',
    'I5',
    'A6',
    'L2',
    'S7',
    'M5',
    'I6',
    'O4',
    'K7',
    'P3',
    'A7',
    'M6',
    'L3',
    'S8',
    'I7',
    'O5',
    'K8',
    'P4',
    'M7',
    'A8',
    'L4',
    'O6',
    'I8',
    'P5',
    'M8',
    'O7',
    'L5',
    'O8',
    'P6',
    'P7',
    'L6',
    'P8',
    'L7',
    'L8',
)
MARK = jax.ShapeDtypeStruct((8, 128), jnp.float32)
KINDS = 3
SLOT_TOTAL = 4
ROWS_Z = 4
LINK_CAP = 8
AT_MID, AT_OUT, AT_PARTNER, AT_OWN, TABLE = 0, 8, 16, 20, 32
KEEP, SIDE, FAR_KEEP, FAR_SIDE, MID, OUT, CODES = 0, 2, 4, 6, 8, 16, 24
NEAR_CODES, FAR_CODES, MID_CODES, OUT_CODES = (0, 4), (4, 8), (8, 16), (16, 24)


def route_kernel(here_ref, placement_ref, row_count_ref, table_ref, *, owners, hid_total, block_rows):
    hid, ep = here_ref[0], here_ref[1]
    z, y = ep // 2, ep % 2
    experts = placement_ref.shape[0]
    pieces = [(e, s) for e in range(experts) for s in range(owners)]
    owner = {}
    for e in range(experts):
        start = jnp.int32(0)
        found = [jnp.int32(0)] * owners
        for j in range(owners):
            o = placement_ref[e, j]
            stop = start + row_count_ref[e, o] // block_rows
            for s in range(owners):
                q = s * hid_total + hid
                found[s] = jnp.where((start <= q) & (q < stop), o, found[s])
            start = stop
        for s in range(owners):
            owner[e, s] = found[s]
    upper = z >= 2
    mid_row = (z == 1) | (z == 2)

    def half(row):
        return row >= 2

    zero = jnp.int32(0)
    mid_in, mid_out, out_in, out_out = zero, zero, zero, zero
    for i in range(TABLE):
        table_ref[i] = jnp.int32(-1)
    mine, partner = zero, zero
    for e, s in pieces:
        row, side = s // 2, s % 2
        o = owner[e, s]
        drow = o // 2
        goes_up, goes_down = drow >= 2, drow < 2
        crosses = goes_up if row < 2 else goes_down
        from_here_half = jnp.logical_not(upper) if row < 2 else upper
        leaves_mid = crosses & from_here_half
        enters_mid = crosses & jnp.logical_not(from_here_half)
        to_top = (drow == ROWS_Z - 1) if row < ROWS_Z - 1 else jnp.bool_(False)
        to_bottom = (drow == 0) if row > 0 else jnp.bool_(False)
        on_outer = jnp.where(upper, to_top, to_bottom)
        near_far = z == row
        outer_row = jnp.where(upper, ROWS_Z - 1, 0)
        from_outer = mid_row & (outer_row == row)
        code = jnp.where(
            near_far,
            jnp.where(y == side, KEEP + e, SIDE + e),
            jnp.where(
                from_outer,
                jnp.where(y == side, FAR_KEEP + e, FAR_SIDE + e),
                jnp.where(mid_row, MID + mid_in, OUT + out_in),
            ),
        )

        @pl.when(leaves_mid & mid_row)
        def _(mid_out=mid_out, code=code):
            table_ref[AT_MID + mid_out] = code

        @pl.when(on_outer & mid_row)
        def _(out_in=out_in, code=code):
            table_ref[AT_OUT + out_in] = code

        is_mine = o == ep
        is_partner = (drow == z) & (o != ep)

        @pl.when(is_mine)
        def _(mine=mine, code=code):
            table_ref[AT_OWN + mine] = code

        @pl.when(is_partner)
        def _(partner=partner, code=code):
            table_ref[AT_PARTNER + partner] = code

        mid_out = mid_out + leaves_mid.astype(jnp.int32)
        mid_in = mid_in + enters_mid.astype(jnp.int32)
        out_in = out_in + on_outer.astype(jnp.int32)
        mine = mine + is_mine.astype(jnp.int32)
        partner = partner + is_partner.astype(jnp.int32)


def route(here, placement, row_count, hid_total, block_rows):
    smem = pl.BlockSpec(memory_space=pltpu.SMEM)
    return pl.pallas_call(
        functools.partial(
            route_kernel,
            owners=placement.shape[1],
            hid_total=hid_total,
            block_rows=block_rows,
        ),
        out_shape=jax.ShapeDtypeStruct((TABLE,), jnp.int32),
        in_specs=[smem] * 3,
        out_specs=smem,
        compiler_params=pltpu.CompilerParams(vmem_limit_bytes=MOVE_VMEM),
        name="route",
    )(here, placement, row_count)


ANYWHERE = pl.BlockSpec(memory_space=pl.ANY)
ON_SMEM = pl.BlockSpec(memory_space=pltpu.SMEM)
ON_VMEM = pl.BlockSpec(memory_space=pltpu.VMEM)
ON_HBM = pl.BlockSpec(memory_space=pltpu.HBM)
TILE = 256


def gather_rows_kernel(gate_ref, up_ref, down_ref, out_ref):
    rows = out_ref.shape[4]
    for kind, ref in enumerate((gate_ref, up_ref, down_ref)):
        block = ref[0] if kind == 2 else ref[0].T
        for x in range(2):
            for core in range(2):
                first = (2 * x + core) * rows
                out_ref[core, x, 0, kind] = block[first : first + rows]


def gather_rows(gate_proj, up_proj, down_proj):
    experts, depth, local_rows = gate_proj.shape
    block_rows = local_rows // 4
    across = pl.BlockSpec((1, depth, local_rows), lambda e: (e, 0, 0))
    along = pl.BlockSpec((1, local_rows, depth), lambda e: (e, 0, 0))
    rows = pl.pallas_call(
        gather_rows_kernel,
        out_shape=jax.ShapeDtypeStruct((2, 2, experts, KINDS, block_rows, depth), jnp.bfloat16),
        grid=(experts,),
        in_specs=[across, across, along],
        out_specs=pl.BlockSpec(
            (2, 2, 1, KINDS, block_rows, depth), lambda e: (0, 0, e, 0, 0, 0)
        ),
        compiler_params=pltpu.CompilerParams(vmem_limit_bytes=32 * 2**20),
        name="gather_rows",
    )(gate_proj, up_proj, down_proj)
    return rows.reshape(2, 2 * experts * KINDS * block_rows, depth)


def product(here_ref, lhs_ref, rot_ref, tile_ref, sems, column):
    step, total = pl.program_id(0), pl.num_programs(0)

    def tile_copy(index):
        slot = lax.rem(index, 2)
        columns = pl.ds(pl.multiple_of(column + index * TILE, TILE), TILE)
        return pltpu.make_async_copy(rot_ref.at[:, columns], tile_ref.at[slot], sems.at[slot])

    @pl.when(step == 0)
    def _():
        tile_copy(step).start()

    @pl.when(step + 1 < total)
    def _():
        tile_copy(step + 1).start()

    tile_copy(step).wait()
    return jnp.dot(
        lhs_ref[0], tile_ref[lax.rem(step, 2)], preferred_element_type=jnp.float32
    )


def send_kernel(here_ref, lhs_ref, rot_ref, after_ref, out_ref, mark_ref, *scratch, column):
    total = product(here_ref, lhs_ref, rot_ref, *scratch, column)
    out_ref[...] = total.astype(jnp.bfloat16)


def keep_kernel(
    here_ref, lhs_ref, rot_ref, recv_ref, after_ref, away_ref, home_ref, mark_ref, *scratch, column
):
    rows = away_ref.shape[0]
    total = product(here_ref, lhs_ref, rot_ref, *scratch, column)
    total = (total + recv_ref[...].astype(jnp.float32)).astype(jnp.bfloat16)
    x = here_ref[0] // 2

    @pl.when(x == 0)
    def _():
        home_ref[...] = total[:rows]
        away_ref[...] = total[rows:]

    @pl.when(x == 1)
    def _():
        home_ref[...] = total[rows:]
        away_ref[...] = total[:rows]


def lhs_spec(lhs, send):
    _, rows, depth = lhs.shape

    def lhs_map(tile, here):
        core = here[0] % 2
        return (1 - core if send else core, 0, 0)

    return pl.BlockSpec((1, rows, depth), lhs_map, pipeline_mode=pl.Buffered(1))


def tile_scratch(depth):
    return [pltpu.VMEM((2, depth, TILE), jnp.bfloat16), pltpu.SemaphoreType.DMA((2,))]


def matmul_send(here, lhs, rotation, column, width, after, cost):
    _, rows, depth = lhs.shape
    return pl.pallas_call(
        functools.partial(send_kernel, column=column),
        out_shape=(jax.ShapeDtypeStruct((rows, width), jnp.bfloat16), MARK),
        grid_spec=pltpu.PrefetchScalarGridSpec(
            num_scalar_prefetch=1,
            grid=(width // TILE,),
            in_specs=[lhs_spec(lhs, True), ON_HBM, ANYWHERE],
            out_specs=(pl.BlockSpec((rows, TILE), lambda t, here: (0, t)), ANYWHERE),
            scratch_shapes=tile_scratch(depth),
        ),
        compiler_params=pltpu.CompilerParams(vmem_limit_bytes=MATMUL_VMEM),
        cost_estimate=cost,
        name="matmul_send",
    )(here, lhs, rotation, after)


def matmul_keep(here, lhs, rotation, recv, column, width, after, cost):
    _, rows, depth = lhs.shape
    out = jax.ShapeDtypeStruct((rows // 2, width), jnp.bfloat16)
    out_spec = pl.BlockSpec((rows // 2, TILE), lambda t, here: (0, t))
    recv_spec = pl.BlockSpec((rows, TILE), lambda t, here: (0, t))
    return pl.pallas_call(
        functools.partial(keep_kernel, column=column),
        out_shape=(out, out, MARK),
        grid_spec=pltpu.PrefetchScalarGridSpec(
            num_scalar_prefetch=1,
            grid=(width // TILE,),
            in_specs=[lhs_spec(lhs, False), ON_HBM, recv_spec, ANYWHERE],
            out_specs=(out_spec, out_spec, ANYWHERE),
            scratch_shapes=tile_scratch(depth),
        ),
        compiler_params=pltpu.CompilerParams(vmem_limit_bytes=MATMUL_VMEM),
        cost_estimate=cost,
        name="matmul_keep",
    )(here, lhs, rotation, recv, after)


def add_kernel(here_ref, home_ref, recv_ref, after_ref, side_ref, keep_ref, mark_ref):
    width = side_ref.shape[1]
    y = here_ref[1] % 2
    for half, ref in ((1 - y, side_ref), (y, keep_ref)):
        part = pl.ds(pl.multiple_of(half * width, 128), width)
        total = home_ref[:, part].astype(jnp.float32) + recv_ref[:, part].astype(jnp.float32)
        ref[...] = total.astype(jnp.bfloat16)


def add(here, home, recv, after, cost):
    rows, width = home.shape
    tile = 128
    out = jax.ShapeDtypeStruct((rows, width // 2), jnp.bfloat16)
    in_spec = pl.BlockSpec((tile, width), lambda i, here: (i, 0))
    out_spec = pl.BlockSpec((tile, width // 2), lambda i, here: (i, 0))
    return pl.pallas_call(
        add_kernel,
        out_shape=(out, out, MARK),
        grid_spec=pltpu.PrefetchScalarGridSpec(
            num_scalar_prefetch=1,
            grid=(rows // tile,),
            in_specs=[in_spec, in_spec, ANYWHERE],
            out_specs=(out_spec, out_spec, ANYWHERE),
        ),
        compiler_params=pltpu.CompilerParams(vmem_limit_bytes=MOVE_VMEM),
        cost_estimate=cost,
        name="add",
    )(here, home, recv, after)


def start_pick(code, bases, sources, target, sem):
    for source, (low, high) in zip(sources, bases):

        @pl.when((code >= low) & (code < high))
        def _(source=source, low=low):
            pltpu.make_async_copy(source.at[code - low], target, sem).start()


def pick_kernel(table_ref, *refs, first, bases):
    sources, out_ref, sems = refs[: len(bases)], refs[-3], refs[-1]
    total = out_ref.shape[0]
    for i in range(total):
        start_pick(table_ref[first + i], bases, sources, out_ref.at[i], sems.at[i])
    for i in range(total):

        @pl.when(table_ref[first + i] >= 0)
        def _(i=i):
            pltpu.make_async_copy(sources[0].at[0], out_ref.at[i], sems.at[i]).wait()


def pick(table, sources, bases, first, total, after, cost):
    piece = sources[0].shape[1:]
    return pl.pallas_call(
        functools.partial(pick_kernel, first=first, bases=bases),
        out_shape=(jax.ShapeDtypeStruct((total,) + piece, jnp.bfloat16), MARK),
        in_specs=[ON_SMEM] + [ANYWHERE] * (len(sources) + 1),
        out_specs=(ON_VMEM, ANYWHERE),
        scratch_shapes=[pltpu.SemaphoreType.DMA((total,))],
        cost_estimate=cost,
        compiler_params=pltpu.CompilerParams(vmem_limit_bytes=MOVE_VMEM),
        name="pick",
    )(table, *sources, after)


def pack_kernel(keep_ref, side_ref, after_ref, out_ref, mark_ref, sems):
    experts = keep_ref.shape[0]
    copies = [
        pltpu.make_async_copy(ref, out_ref.at[pl.ds(n * experts, experts)], sems.at[n])
        for n, ref in enumerate((keep_ref, side_ref))
    ]
    for copy in copies:
        copy.start()
    for copy in copies:
        copy.wait()


def pack(keep, side, after, cost):
    experts = keep.shape[0]
    return pl.pallas_call(
        pack_kernel,
        out_shape=(jax.ShapeDtypeStruct((2 * experts,) + keep.shape[1:], jnp.bfloat16), MARK),
        in_specs=[ANYWHERE] * 3,
        out_specs=(ON_VMEM, ANYWHERE),
        scratch_shapes=[pltpu.SemaphoreType.DMA((2,))],
        compiler_params=pltpu.CompilerParams(vmem_limit_bytes=MOVE_VMEM),
        cost_estimate=cost,
        name="pack",
    )(keep, side, after)


def place_kernel(here_ref, table_ref, *refs, bases, column):
    sources, partner_ref = refs[: len(bases)], refs[len(bases)]
    out_ref, mark_ref, held_ref, in_sems, out_sems = refs[-5:]
    _, _, _, rows, width = held_ref.shape
    y = here_ref[1] % 2

    def target(slot, half):
        at = pl.multiple_of(column + half * width, 128)
        return out_ref.at[:, pl.ds(slot * rows, rows), pl.ds(at, width)]

    for slot in range(SLOT_TOTAL):
        code = table_ref[AT_OWN + slot]
        start_pick(code, bases, sources, held_ref.at[slot, 0], in_sems.at[slot, 0])

        @pl.when(code >= 0)
        def _(slot=slot):
            pltpu.make_async_copy(
                partner_ref.at[slot], held_ref.at[slot, 1], in_sems.at[slot, 1]
            ).start()

        @pl.when(code < 0)
        def _(slot=slot):
            held_ref[slot] = jnp.zeros(held_ref.shape[1:], held_ref.dtype)

    for slot in range(SLOT_TOTAL):

        @pl.when(table_ref[AT_OWN + slot] >= 0)
        def _(slot=slot):
            for part in range(2):
                pltpu.make_async_copy(
                    partner_ref.at[slot], held_ref.at[slot, part], in_sems.at[slot, part]
                ).wait()

        pltpu.make_async_copy(held_ref.at[slot, 0], target(slot, y), out_sems.at[slot, 0]).start()
        pltpu.make_async_copy(
            held_ref.at[slot, 1], target(slot, 1 - y), out_sems.at[slot, 1]
        ).start()
    for slot in range(SLOT_TOTAL):
        pltpu.make_async_copy(held_ref.at[slot, 0], target(slot, y), out_sems.at[slot, 0]).wait()
        pltpu.make_async_copy(
            held_ref.at[slot, 1], target(slot, 1 - y), out_sems.at[slot, 1]
        ).wait()


def place(here, table, sources, bases, partner, column, full_width, previous, after, cost):
    piece = partner.shape[1:]
    operands = [here, table, *sources, partner, after]
    in_specs = [ON_SMEM, ON_SMEM] + [ANYWHERE] * (len(sources) + 2)
    aliases = {}
    if previous is not None:
        aliases = {len(operands): 0}
        operands.append(previous)
        in_specs.append(ANYWHERE)
    return pl.pallas_call(
        functools.partial(place_kernel, bases=bases, column=column),
        out_shape=(
            jax.ShapeDtypeStruct((KINDS, SLOT_TOTAL * piece[1], full_width), jnp.bfloat16),
            MARK,
        ),
        in_specs=in_specs,
        out_specs=(ANYWHERE, ANYWHERE),
        scratch_shapes=[
            pltpu.VMEM((SLOT_TOTAL, 2) + piece, jnp.bfloat16),
            pltpu.SemaphoreType.DMA((SLOT_TOTAL, 2)),
            pltpu.SemaphoreType.DMA((SLOT_TOTAL, 2)),
        ],
        input_output_aliases=aliases,
        cost_estimate=cost,
        compiler_params=pltpu.CompilerParams(vmem_limit_bytes=MOVE_VMEM),
        name="place",
    )(*operands)


def pipelined(gate_proj, up_proj, down_proj, rotation, placement, row_count):
    hid_total = lax.axis_size("hid")
    experts, depth, local_rows = gate_proj.shape
    full_width = rotation.shape[1]
    block_rows = local_rows // hid_total
    here = jnp.stack([lax.axis_index("hid"), lax.axis_index("ep")]).astype(jnp.int32)
    table = route(here, placement, row_count, hid_total, block_rows)

    lhs = gather_rows(gate_proj, up_proj, down_proj)

    cores = [(h, h ^ 1) for h in range(4)]
    along_x = [(h, h ^ 2) for h in range(4)]
    along_y = [(s, s ^ 1) for s in range(8)]
    inward = [(0, 2), (1, 3), (6, 4), (7, 5)]
    middle = [(2, 4), (3, 5), (4, 2), (5, 3)]
    outward = [(4, 6), (5, 7), (2, 0), (3, 1)]
    widths = [2 * tiles * TILE for tiles in CHUNK_TILES]
    columns = [sum(widths[:i]) for i in range(len(widths))]
    chunks = len(widths)

    core_recv, x_recv, home, keep, side = {}, {}, {}, {}, {}
    near, far, mid, outer, partner = {}, {}, {}, {}, {}
    all_codes = [NEAR_CODES, FAR_CODES, MID_CODES, OUT_CODES]

    def send_terms(i, served, *order):
        sent, mark = matmul_send(here, lhs, rotation, columns[i], widths[i], *order)
        core_recv[i] = lax.ppermute(sent, "hid", cores)
        return served, mark

    def keep_terms(i, served, *order):
        recv = core_recv.pop(i)
        away, home[i], mark = matmul_keep(here, lhs, rotation, recv, columns[i], widths[i], *order)
        x_recv[i] = lax.ppermute(away, "hid", along_x)
        return served, mark

    def sum_terms(i, served, *order):
        pieces = (experts, KINDS, block_rows, widths[i] // 2)
        out, own, mark = add(here, home.pop(i), x_recv.pop(i), *order)
        keep[i] = own.reshape(pieces)
        side[i] = lax.ppermute(out.reshape(pieces), "ep", along_y)
        return served, mark

    def send_inward(i, served, *order):
        near[i], mark = pack(keep.pop(i), side.pop(i), *order)
        far[i] = lax.ppermute(near[i], "ep", inward)
        return served, mark

    def send_across(i, served, *order):
        codes = [NEAR_CODES, FAR_CODES]
        out, mark = pick(table, [near[i], far[i]], codes, AT_MID, LINK_CAP, *order)
        mid[i] = lax.ppermute(out, "ep", middle)
        return served, mark

    def send_outward(i, served, *order):
        codes = [NEAR_CODES, MID_CODES]
        out, mark = pick(table, [near[i], mid[i]], codes, AT_OUT, LINK_CAP, *order)
        outer[i] = lax.ppermute(out, "ep", outward)
        return served, mark

    def send_partner(i, served, *order):
        sources = [near[i], far[i], mid[i], outer[i]]
        out, mark = pick(table, sources, all_codes, AT_PARTNER, SLOT_TOTAL, *order)
        partner[i] = lax.ppermute(out, "ep", along_y)
        return served, mark

    def put(i, served, *order):
        sources = [near.pop(i), far.pop(i), mid.pop(i), outer.pop(i)]
        return place(
            here, table, sources, all_codes, partner.pop(i), columns[i], full_width, served, *order
        )

    stages = dict(
        S=send_terms,
        K=keep_terms,
        A=sum_terms,
        I=send_inward,
        M=send_across,
        O=send_outward,
        P=send_partner,
        L=put,
    )
    served, mark = None, here
    for step in ORDER:
        served, mark = stages[step[0]](int(step[1:]), served, mark, COST)
    return served.transpose(1, 0, 2)[None]


def count_below(bound, residue, shard_total):
    return (bound + shard_total - 1 - residue) // shard_total


def routing(placement, row_count, block_rows):
    owner_total = placement.shape[1]
    blocks = row_count // block_rows
    onehot = (
        placement[:, :, None] == jnp.arange(owner_total, dtype=jnp.int32)[None, None, :]
    ).astype(jnp.int32)
    ordered = jnp.sum(onehot * blocks[:, None, :], axis=2)
    ordered_start = jnp.cumsum(ordered, axis=1) - ordered
    first_block = jnp.sum(onehot * ordered_start[:, :, None], axis=1)
    return (blocks, first_block)


def assemble(received, received_slot, slot_blocks, experts):
    flat_slot = received_slot.reshape(-1)
    matches = flat_slot[None, :] == jnp.arange(slot_blocks, dtype=jnp.int32)[:, None]
    present = jnp.any(matches, axis=1)
    picked = jnp.argmax(matches, axis=1)
    source_ids = picked // experts
    expert_ids = picked % experts
    chosen = received[source_ids, :, expert_ids]
    chosen = jnp.where(present[:, None, None, None], chosen, jnp.zeros((), jnp.bfloat16))
    return chosen.reshape(1, slot_blocks * chosen.shape[1], chosen.shape[2], chosen.shape[3])


def gathered(gate_proj, up_proj, down_proj, rotation, placement, row_count):
    shard_total = lax.axis_size("hid")
    owner_total = lax.axis_size("ep")
    experts, width_part, local_rows = gate_proj.shape
    full_width = rotation.shape[1]
    block_rows = local_rows // shard_total
    stacked = jnp.stack(
        [
            jnp.transpose(gate_proj, (2, 0, 1)),
            jnp.transpose(up_proj, (2, 0, 1)),
            jnp.transpose(down_proj, (1, 0, 2)),
        ],
        axis=2,
    )
    stacked = stacked.reshape(local_rows, experts * 3, width_part)
    summed = lax.psum_scatter(
        jnp.einsum("fck,kh->fch", stacked, rotation, preferred_element_type=jnp.float32).astype(
            jnp.bfloat16
        ),
        "hid",
        scatter_dimension=0,
        tiled=True,
    )
    rotated = summed.reshape(block_rows, experts, 3, full_width)
    shard_here = lax.axis_index("hid")
    owner_here = lax.axis_index("ep")
    block_here = owner_here * shard_total + shard_here
    blocks, first_block = routing(placement, row_count, block_rows)
    inside = ((first_block <= block_here) & (block_here < first_block + blocks)).astype(jnp.int32)
    owner_ids = jnp.arange(owner_total, dtype=jnp.int32)
    target_owner = jnp.sum(inside * owner_ids[None, :], axis=1)
    at_shard = count_below(first_block + blocks, shard_here, shard_total) - count_below(
        first_block, shard_here, shard_total
    )
    offset = jnp.cumsum(at_shard, axis=0) - at_shard
    slot_index = jnp.sum(
        inside * (offset - count_below(first_block, shard_here, shard_total)), axis=1
    )
    slot_index = slot_index + count_below(block_here, shard_here, shard_total)
    slot_blocks = 2 * experts
    all_blocks, all_owner, all_slot = (
        lax.all_gather(rotated[None], "ep", axis=0, tiled=True),
        lax.all_gather(target_owner[None], "ep", axis=0, tiled=True),
        lax.all_gather(slot_index[None], "ep", axis=0, tiled=True),
    )
    received_slot = jnp.where(all_owner == owner_here, all_slot, -1)
    return assemble(all_blocks, received_slot, slot_blocks, experts)


def solution(mesh):
    in_specs = (
        P(None, "hid", "ep"),
        P(None, "hid", "ep"),
        P(None, "ep", "hid"),
        P("hid", None),
        P(),
        P(),
    )
    out_specs = P("ep", "hid", None, None)
    fits = mesh.shape["hid"] == 4 and mesh.shape["ep"] == 8
    return jax.shard_map(
        pipelined if fits else gathered,
        mesh=mesh,
        in_specs=in_specs,
        out_specs=out_specs,
        check_vma=False,
    )
```

```python
import functools

import jax
import jax.numpy as jnp
from jax import lax
from jax.experimental import pallas as pl
from jax.experimental.pallas import tpu as pltpu
from jax.sharding import PartitionSpec as P

CHUNK_TILES = (1, 1, 2, 2, 2, 2, 2, 1, 1)
MATMUL_VMEM = 36 * 2**20
MOVE_VMEM = 8 * 2**20
COST = pl.CostEstimate(flops=25000000000, bytes_accessed=2**10, transcendentals=0)
ORDER = (
    'S0',
    'K0',
    'S1',
    'S2',
    'K1',
    'K2',
    'A0',
    'S3',
    'A1',
    'I0',
    'K3',
    'I1',
    'M0',
    'A2',
    'S4',
    'M1',
    'I2',
    'K4',
    'O0',
    'A3',
    'M2',
    'I3',
    'O1',
    'A4',
    'P0',
    'I4',
    'M3',
    'P1',
    'L0',
    'S5',
    'O2',
    'L1',
    'K5',
    'S6',
    'M4',
    'K6',
    'A5',
    'O3',
    'P2',
    'I5',
    'A6',
    'L2',
    'S7',
    'M5',
    'I6',
    'O4',
    'K7',
    'P3',
    'A7',
    'M6',
    'L3',
    'S8',
    'I7',
    'O5',
    'K8',
    'P4',
    'M7',
    'A8',
    'L4',
    'O6',
    'I8',
    'P5',
    'M8',
    'O7',
    'L5',
    'O8',
    'P6',
    'P7',
    'L6',
    'P8',
    'L7',
    'L8',
)
MARK = jax.ShapeDtypeStruct((8, 128), jnp.float32)
KINDS = 3
SLOT_TOTAL = 4
ROWS_Z = 4
LINK_CAP = 8
AT_MID, AT_OUT, AT_PARTNER, AT_OWN, TABLE = 0, 8, 16, 20, 32
KEEP, SIDE, FAR_KEEP, FAR_SIDE, MID, OUT, CODES = 0, 2, 4, 6, 8, 16, 24
NEAR_CODES, FAR_CODES, MID_CODES, OUT_CODES = (0, 4), (4, 8), (8, 16), (16, 24)


def route_kernel(here_ref, placement_ref, row_count_ref, table_ref, *, owners, hid_total, block_rows):
    hid, ep = here_ref[0], here_ref[1]
    z, y = ep // 2, ep % 2
    experts = placement_ref.shape[0]
    pieces = [(e, s) for e in range(experts) for s in range(owners)]
    owner = {}
    for e in range(experts):
        start = jnp.int32(0)
        found = [jnp.int32(0)] * owners
        for j in range(owners):
            o = placement_ref[e, j]
            stop = start + row_count_ref[e, o] // block_rows
            for s in range(owners):
                q = s * hid_total + hid
                found[s] = jnp.where((start <= q) & (q < stop), o, found[s])
            start = stop
        for s in range(owners):
            owner[e, s] = found[s]
    upper = z >= 2
    mid_row = (z == 1) | (z == 2)

    def half(row):
        return row >= 2

    zero = jnp.int32(0)
    mid_in, mid_out, out_in, out_out = zero, zero, zero, zero
    for i in range(TABLE):
        table_ref[i] = jnp.int32(-1)
    mine, partner = zero, zero
    for e, s in pieces:
        row, side = s // 2, s % 2
        o = owner[e, s]
        drow = o // 2
        goes_up, goes_down = drow >= 2, drow < 2
        crosses = goes_up if row < 2 else goes_down
        from_here_half = jnp.logical_not(upper) if row < 2 else upper
        leaves_mid = crosses & from_here_half
        enters_mid = crosses & jnp.logical_not(from_here_half)
        to_top = (drow == ROWS_Z - 1) if row < ROWS_Z - 1 else jnp.bool_(False)
        to_bottom = (drow == 0) if row > 0 else jnp.bool_(False)
        on_outer = jnp.where(upper, to_top, to_bottom)
        near_far = z == row
        outer_row = jnp.where(upper, ROWS_Z - 1, 0)
        from_outer = mid_row & (outer_row == row)
        code = jnp.where(
            near_far,
            jnp.where(y == side, KEEP + e, SIDE + e),
            jnp.where(
                from_outer,
                jnp.where(y == side, FAR_KEEP + e, FAR_SIDE + e),
                jnp.where(mid_row, MID + mid_in, OUT + out_in),
            ),
        )

        @pl.when(leaves_mid & mid_row)
        def _(mid_out=mid_out, code=code):
            table_ref[AT_MID + mid_out] = code

        @pl.when(on_outer & mid_row)
        def _(out_in=out_in, code=code):
            table_ref[AT_OUT + out_in] = code

        is_mine = o == ep
        is_partner = (drow == z) & (o != ep)

        @pl.when(is_mine)
        def _(mine=mine, code=code):
            table_ref[AT_OWN + mine] = code

        @pl.when(is_partner)
        def _(partner=partner, code=code):
            table_ref[AT_PARTNER + partner] = code

        mid_out = mid_out + leaves_mid.astype(jnp.int32)
        mid_in = mid_in + enters_mid.astype(jnp.int32)
        out_in = out_in + on_outer.astype(jnp.int32)
        mine = mine + is_mine.astype(jnp.int32)
        partner = partner + is_partner.astype(jnp.int32)


def route(here, placement, row_count, hid_total, block_rows):
    smem = pl.BlockSpec(memory_space=pltpu.SMEM)
    return pl.pallas_call(
        functools.partial(
            route_kernel,
            owners=placement.shape[1],
            hid_total=hid_total,
            block_rows=block_rows,
        ),
        out_shape=jax.ShapeDtypeStruct((TABLE,), jnp.int32),
        in_specs=[smem] * 3,
        out_specs=smem,
        compiler_params=pltpu.CompilerParams(vmem_limit_bytes=MOVE_VMEM),
        name="route",
    )(here, placement, row_count)


ANYWHERE = pl.BlockSpec(memory_space=pl.ANY)
ON_SMEM = pl.BlockSpec(memory_space=pltpu.SMEM)
ON_VMEM = pl.BlockSpec(memory_space=pltpu.VMEM)
ON_HBM = pl.BlockSpec(memory_space=pltpu.HBM)
TILE = 256


def gather_rows_kernel(gate_ref, up_ref, down_ref, out_ref):
    rows = out_ref.shape[4]
    for kind, ref in enumerate((gate_ref, up_ref, down_ref)):
        block = ref[0] if kind == 2 else ref[0].T
        for x in range(2):
            for core in range(2):
                first = (2 * x + core) * rows
                out_ref[core, x, 0, kind] = block[first : first + rows]


def gather_rows(gate_proj, up_proj, down_proj):
    experts, depth, local_rows = gate_proj.shape
    block_rows = local_rows // 4
    across = pl.BlockSpec((1, depth, local_rows), lambda e: (e, 0, 0))
    along = pl.BlockSpec((1, local_rows, depth), lambda e: (e, 0, 0))
    rows = pl.pallas_call(
        gather_rows_kernel,
        out_shape=jax.ShapeDtypeStruct((2, 2, experts, KINDS, block_rows, depth), jnp.bfloat16),
        grid=(experts,),
        in_specs=[across, across, along],
        out_specs=pl.BlockSpec(
            (2, 2, 1, KINDS, block_rows, depth), lambda e: (0, 0, e, 0, 0, 0)
        ),
        compiler_params=pltpu.CompilerParams(vmem_limit_bytes=32 * 2**20),
        name="gather_rows",
    )(gate_proj, up_proj, down_proj)
    return rows.reshape(2, 2 * experts * KINDS * block_rows, depth)


def product(here_ref, lhs_ref, rot_ref, tile_ref, sems, column):
    step, total = pl.program_id(0), pl.num_programs(0)

    def tile_copy(index):
        slot = lax.rem(index, 2)
        columns = pl.ds(pl.multiple_of(column + index * TILE, TILE), TILE)
        return pltpu.make_async_copy(rot_ref.at[:, columns], tile_ref.at[slot], sems.at[slot])

    @pl.when(step == 0)
    def _():
        tile_copy(step).start()

    @pl.when(step + 1 < total)
    def _():
        tile_copy(step + 1).start()

    tile_copy(step).wait()
    return jnp.dot(
        lhs_ref[0], tile_ref[lax.rem(step, 2)], preferred_element_type=jnp.float32
    )


def send_kernel(here_ref, lhs_ref, rot_ref, after_ref, out_ref, mark_ref, *scratch, column):
    total = product(here_ref, lhs_ref, rot_ref, *scratch, column)
    out_ref[...] = total.astype(jnp.bfloat16)


def keep_kernel(
    here_ref, lhs_ref, rot_ref, recv_ref, after_ref, away_ref, home_ref, mark_ref, *scratch, column
):
    rows = away_ref.shape[0]
    total = product(here_ref, lhs_ref, rot_ref, *scratch, column)
    total = (total + recv_ref[...].astype(jnp.float32)).astype(jnp.bfloat16)
    x = here_ref[0] // 2

    @pl.when(x == 0)
    def _():
        home_ref[...] = total[:rows]
        away_ref[...] = total[rows:]

    @pl.when(x == 1)
    def _():
        home_ref[...] = total[rows:]
        away_ref[...] = total[:rows]


def lhs_spec(lhs, send):
    _, rows, depth = lhs.shape

    def lhs_map(tile, here):
        core = here[0] % 2
        return (1 - core if send else core, 0, 0)

    return pl.BlockSpec((1, rows, depth), lhs_map, pipeline_mode=pl.Buffered(1))


def tile_scratch(depth):
    return [pltpu.VMEM((2, depth, TILE), jnp.bfloat16), pltpu.SemaphoreType.DMA((2,))]


def matmul_send(here, lhs, rotation, column, width, after, cost):
    _, rows, depth = lhs.shape
    return pl.pallas_call(
        functools.partial(send_kernel, column=column),
        out_shape=(jax.ShapeDtypeStruct((rows, width), jnp.bfloat16), MARK),
        grid_spec=pltpu.PrefetchScalarGridSpec(
            num_scalar_prefetch=1,
            grid=(width // TILE,),
            in_specs=[lhs_spec(lhs, True), ON_HBM, ANYWHERE],
            out_specs=(pl.BlockSpec((rows, TILE), lambda t, here: (0, t)), ANYWHERE),
            scratch_shapes=tile_scratch(depth),
        ),
        compiler_params=pltpu.CompilerParams(vmem_limit_bytes=MATMUL_VMEM),
        cost_estimate=cost,
        name="matmul_send",
    )(here, lhs, rotation, after)


def matmul_keep(here, lhs, rotation, recv, column, width, after, cost):
    _, rows, depth = lhs.shape
    out = jax.ShapeDtypeStruct((rows // 2, width), jnp.bfloat16)
    out_spec = pl.BlockSpec((rows // 2, TILE), lambda t, here: (0, t))
    recv_spec = pl.BlockSpec((rows, TILE), lambda t, here: (0, t))
    return pl.pallas_call(
        functools.partial(keep_kernel, column=column),
        out_shape=(out, out, MARK),
        grid_spec=pltpu.PrefetchScalarGridSpec(
            num_scalar_prefetch=1,
            grid=(width // TILE,),
            in_specs=[lhs_spec(lhs, False), ON_HBM, recv_spec, ANYWHERE],
            out_specs=(out_spec, out_spec, ANYWHERE),
            scratch_shapes=tile_scratch(depth),
        ),
        compiler_params=pltpu.CompilerParams(vmem_limit_bytes=MATMUL_VMEM),
        cost_estimate=cost,
        name="matmul_keep",
    )(here, lhs, rotation, recv, after)


def add_kernel(here_ref, home_ref, recv_ref, after_ref, side_ref, keep_ref, mark_ref):
    width = side_ref.shape[1]
    y = here_ref[1] % 2
    for half, ref in ((1 - y, side_ref), (y, keep_ref)):
        part = pl.ds(pl.multiple_of(half * width, 128), width)
        total = home_ref[:, part].astype(jnp.float32) + recv_ref[:, part].astype(jnp.float32)
        ref[...] = total.astype(jnp.bfloat16)


def add(here, home, recv, after, cost):
    rows, width = home.shape
    tile = 128
    out = jax.ShapeDtypeStruct((rows, width // 2), jnp.bfloat16)
    in_spec = pl.BlockSpec((tile, width), lambda i, here: (i, 0))
    out_spec = pl.BlockSpec((tile, width // 2), lambda i, here: (i, 0))
    return pl.pallas_call(
        add_kernel,
        out_shape=(out, out, MARK),
        grid_spec=pltpu.PrefetchScalarGridSpec(
            num_scalar_prefetch=1,
            grid=(rows // tile,),
            in_specs=[in_spec, in_spec, ANYWHERE],
            out_specs=(out_spec, out_spec, ANYWHERE),
        ),
        compiler_params=pltpu.CompilerParams(vmem_limit_bytes=MOVE_VMEM),
        cost_estimate=cost,
        name="add",
    )(here, home, recv, after)


def start_pick(code, bases, sources, target, sem):
    for source, (low, high) in zip(sources, bases):

        @pl.when((code >= low) & (code < high))
        def _(source=source, low=low):
            pltpu.make_async_copy(source.at[code - low], target, sem).start()


def pick_kernel(table_ref, *refs, first, bases):
    sources, out_ref, sems = refs[: len(bases)], refs[-3], refs[-1]
    total = out_ref.shape[0]
    for i in range(total):
        start_pick(table_ref[first + i], bases, sources, out_ref.at[i], sems.at[i])
    for i in range(total):

        @pl.when(table_ref[first + i] >= 0)
        def _(i=i):
            pltpu.make_async_copy(sources[0].at[0], out_ref.at[i], sems.at[i]).wait()


def pick(table, sources, bases, first, total, after, cost):
    piece = sources[0].shape[1:]
    return pl.pallas_call(
        functools.partial(pick_kernel, first=first, bases=bases),
        out_shape=(jax.ShapeDtypeStruct((total,) + piece, jnp.bfloat16), MARK),
        in_specs=[ON_SMEM] + [ANYWHERE] * (len(sources) + 1),
        out_specs=(ON_VMEM, ANYWHERE),
        scratch_shapes=[pltpu.SemaphoreType.DMA((total,))],
        cost_estimate=cost,
        compiler_params=pltpu.CompilerParams(vmem_limit_bytes=MOVE_VMEM),
        name="pick",
    )(table, *sources, after)


def pack_kernel(keep_ref, side_ref, after_ref, out_ref, mark_ref, sems):
    experts = keep_ref.shape[0]
    copies = [
        pltpu.make_async_copy(ref, out_ref.at[pl.ds(n * experts, experts)], sems.at[n])
        for n, ref in enumerate((keep_ref, side_ref))
    ]
    for copy in copies:
        copy.start()
    for copy in copies:
        copy.wait()


def pack(keep, side, after, cost):
    experts = keep.shape[0]
    return pl.pallas_call(
        pack_kernel,
        out_shape=(jax.ShapeDtypeStruct((2 * experts,) + keep.shape[1:], jnp.bfloat16), MARK),
        in_specs=[ANYWHERE] * 3,
        out_specs=(ON_VMEM, ANYWHERE),
        scratch_shapes=[pltpu.SemaphoreType.DMA((2,))],
        compiler_params=pltpu.CompilerParams(vmem_limit_bytes=MOVE_VMEM),
        cost_estimate=cost,
        name="pack",
    )(keep, side, after)


def place_kernel(here_ref, table_ref, *refs, bases, column):
    sources, partner_ref = refs[: len(bases)], refs[len(bases)]
    out_ref, mark_ref, held_ref, in_sems, out_sems = refs[-5:]
    _, _, _, rows, width = held_ref.shape
    y = here_ref[1] % 2

    def target(slot, half):
        at = pl.multiple_of(column + half * width, 128)
        return out_ref.at[:, pl.ds(slot * rows, rows), pl.ds(at, width)]

    for slot in range(SLOT_TOTAL):
        code = table_ref[AT_OWN + slot]
        start_pick(code, bases, sources, held_ref.at[slot, 0], in_sems.at[slot, 0])

        @pl.when(code >= 0)
        def _(slot=slot):
            pltpu.make_async_copy(
                partner_ref.at[slot], held_ref.at[slot, 1], in_sems.at[slot, 1]
            ).start()

        @pl.when(code < 0)
        def _(slot=slot):
            held_ref[slot] = jnp.zeros(held_ref.shape[1:], held_ref.dtype)

    for slot in range(SLOT_TOTAL):

        @pl.when(table_ref[AT_OWN + slot] >= 0)
        def _(slot=slot):
            for part in range(2):
                pltpu.make_async_copy(
                    partner_ref.at[slot], held_ref.at[slot, part], in_sems.at[slot, part]
                ).wait()

        pltpu.make_async_copy(held_ref.at[slot, 0], target(slot, y), out_sems.at[slot, 0]).start()
        pltpu.make_async_copy(
            held_ref.at[slot, 1], target(slot, 1 - y), out_sems.at[slot, 1]
        ).start()
    for slot in range(SLOT_TOTAL):
        pltpu.make_async_copy(held_ref.at[slot, 0], target(slot, y), out_sems.at[slot, 0]).wait()
        pltpu.make_async_copy(
            held_ref.at[slot, 1], target(slot, 1 - y), out_sems.at[slot, 1]
        ).wait()


def place(here, table, sources, bases, partner, column, full_width, previous, after, cost):
    piece = partner.shape[1:]
    operands = [here, table, *sources, partner, after]
    in_specs = [ON_SMEM, ON_SMEM] + [ANYWHERE] * (len(sources) + 2)
    aliases = {}
    if previous is not None:
        aliases = {len(operands): 0}
        operands.append(previous)
        in_specs.append(ANYWHERE)
    return pl.pallas_call(
        functools.partial(place_kernel, bases=bases, column=column),
        out_shape=(
            jax.ShapeDtypeStruct((KINDS, SLOT_TOTAL * piece[1], full_width), jnp.bfloat16),
            MARK,
        ),
        in_specs=in_specs,
        out_specs=(ANYWHERE, ANYWHERE),
        scratch_shapes=[
            pltpu.VMEM((SLOT_TOTAL, 2) + piece, jnp.bfloat16),
            pltpu.SemaphoreType.DMA((SLOT_TOTAL, 2)),
            pltpu.SemaphoreType.DMA((SLOT_TOTAL, 2)),
        ],
        input_output_aliases=aliases,
        cost_estimate=cost,
        compiler_params=pltpu.CompilerParams(vmem_limit_bytes=MOVE_VMEM),
        name="place",
    )(*operands)


def pipelined(gate_proj, up_proj, down_proj, rotation, placement, row_count):
    hid_total = lax.axis_size("hid")
    experts, depth, local_rows = gate_proj.shape
    full_width = rotation.shape[1]
    block_rows = local_rows // hid_total
    here = jnp.stack([lax.axis_index("hid"), lax.axis_index("ep")]).astype(jnp.int32)
    table = route(here, placement, row_count, hid_total, block_rows)

    lhs = gather_rows(gate_proj, up_proj, down_proj)

    cores = [(h, h ^ 1) for h in range(4)]
    along_x = [(h, h ^ 2) for h in range(4)]
    along_y = [(s, s ^ 1) for s in range(8)]
    inward = [(0, 2), (1, 3), (6, 4), (7, 5)]
    middle = [(2, 4), (3, 5), (4, 2), (5, 3)]
    outward = [(4, 6), (5, 7), (2, 0), (3, 1)]
    widths = [2 * tiles * TILE for tiles in CHUNK_TILES]
    columns = [sum(widths[:i]) for i in range(len(widths))]
    chunks = len(widths)

    core_recv, x_recv, home, keep, side = {}, {}, {}, {}, {}
    near, far, mid, outer, partner = {}, {}, {}, {}, {}
    all_codes = [NEAR_CODES, FAR_CODES, MID_CODES, OUT_CODES]

    def send_terms(i, served, *order):
        sent, mark = matmul_send(here, lhs, rotation, columns[i], widths[i], *order)
        core_recv[i] = lax.ppermute(sent, "hid", cores)
        return served, mark

    def keep_terms(i, served, *order):
        recv = core_recv.pop(i)
        away, home[i], mark = matmul_keep(here, lhs, rotation, recv, columns[i], widths[i], *order)
        x_recv[i] = lax.ppermute(away, "hid", along_x)
        return served, mark

    def sum_terms(i, served, *order):
        pieces = (experts, KINDS, block_rows, widths[i] // 2)
        out, own, mark = add(here, home.pop(i), x_recv.pop(i), *order)
        keep[i] = own.reshape(pieces)
        side[i] = lax.ppermute(out.reshape(pieces), "ep", along_y)
        return served, mark

    def send_inward(i, served, *order):
        near[i], mark = pack(keep.pop(i), side.pop(i), *order)
        far[i] = lax.ppermute(near[i], "ep", inward)
        return served, mark

    def send_across(i, served, *order):
        codes = [NEAR_CODES, FAR_CODES]
        out, mark = pick(table, [near[i], far[i]], codes, AT_MID, LINK_CAP, *order)
        mid[i] = lax.ppermute(out, "ep", middle)
        return served, mark

    def send_outward(i, served, *order):
        codes = [NEAR_CODES, MID_CODES]
        out, mark = pick(table, [near[i], mid[i]], codes, AT_OUT, LINK_CAP, *order)
        outer[i] = lax.ppermute(out, "ep", outward)
        return served, mark

    def send_partner(i, served, *order):
        sources = [near[i], far[i], mid[i], outer[i]]
        out, mark = pick(table, sources, all_codes, AT_PARTNER, SLOT_TOTAL, *order)
        partner[i] = lax.ppermute(out, "ep", along_y)
        return served, mark

    def put(i, served, *order):
        sources = [near.pop(i), far.pop(i), mid.pop(i), outer.pop(i)]
        return place(
            here, table, sources, all_codes, partner.pop(i), columns[i], full_width, served, *order
        )

    stages = dict(
        S=send_terms,
        K=keep_terms,
        A=sum_terms,
        I=send_inward,
        M=send_across,
        O=send_outward,
        P=send_partner,
        L=put,
    )
    served, mark = None, here
    for step in ORDER:
        served, mark = stages[step[0]](int(step[1:]), served, mark, COST)
    return served.transpose(1, 0, 2)[None]


def count_below(bound, residue, shard_total):
    return (bound + shard_total - 1 - residue) // shard_total


def routing(placement, row_count, block_rows):
    owner_total = placement.shape[1]
    blocks = row_count // block_rows
    onehot = (
        placement[:, :, None] == jnp.arange(owner_total, dtype=jnp.int32)[None, None, :]
    ).astype(jnp.int32)
    ordered = jnp.sum(onehot * blocks[:, None, :], axis=2)
    ordered_start = jnp.cumsum(ordered, axis=1) - ordered
    first_block = jnp.sum(onehot * ordered_start[:, :, None], axis=1)
    return (blocks, first_block)


def assemble(received, received_slot, slot_blocks, experts):
    flat_slot = received_slot.reshape(-1)
    matches = flat_slot[None, :] == jnp.arange(slot_blocks, dtype=jnp.int32)[:, None]
    present = jnp.any(matches, axis=1)
    picked = jnp.argmax(matches, axis=1)
    source_ids = picked // experts
    expert_ids = picked % experts
    chosen = received[source_ids, :, expert_ids]
    chosen = jnp.where(present[:, None, None, None], chosen, jnp.zeros((), jnp.bfloat16))
    return chosen.reshape(1, slot_blocks * chosen.shape[1], chosen.shape[2], chosen.shape[3])


def gathered(gate_proj, up_proj, down_proj, rotation, placement, row_count):
    shard_total = lax.axis_size("hid")
    owner_total = lax.axis_size("ep")
    experts, width_part, local_rows = gate_proj.shape
    full_width = rotation.shape[1]
    block_rows = local_rows // shard_total
    stacked = jnp.stack(
        [
            jnp.transpose(gate_proj, (2, 0, 1)),
            jnp.transpose(up_proj, (2, 0, 1)),
            jnp.transpose(down_proj, (1, 0, 2)),
        ],
        axis=2,
    )
    stacked = stacked.reshape(local_rows, experts * 3, width_part)
    summed = lax.psum_scatter(
        jnp.einsum("fck,kh->fch", stacked, rotation, preferred_element_type=jnp.float32).astype(
            jnp.bfloat16
        ),
        "hid",
        scatter_dimension=0,
        tiled=True,
    )
    rotated = summed.reshape(block_rows, experts, 3, full_width)
    shard_here = lax.axis_index("hid")
    owner_here = lax.axis_index("ep")
    block_here = owner_here * shard_total + shard_here
    blocks, first_block = routing(placement, row_count, block_rows)
    inside = ((first_block <= block_here) & (block_here < first_block + blocks)).astype(jnp.int32)
    owner_ids = jnp.arange(owner_total, dtype=jnp.int32)
    target_owner = jnp.sum(inside * owner_ids[None, :], axis=1)
    at_shard = count_below(first_block + blocks, shard_here, shard_total) - count_below(
        first_block, shard_here, shard_total
    )
    offset = jnp.cumsum(at_shard, axis=0) - at_shard
    slot_index = jnp.sum(
        inside * (offset - count_below(first_block, shard_here, shard_total)), axis=1
    )
    slot_index = slot_index + count_below(block_here, shard_here, shard_total)
    slot_blocks = 2 * experts
    all_blocks, all_owner, all_slot = (
        lax.all_gather(rotated[None], "ep", axis=0, tiled=True),
        lax.all_gather(target_owner[None], "ep", axis=0, tiled=True),
        lax.all_gather(slot_index[None], "ep", axis=0, tiled=True),
    )
    received_slot = jnp.where(all_owner == owner_here, all_slot, -1)
    return assemble(all_blocks, received_slot, slot_blocks, experts)


def solution(mesh):
    in_specs = (
        P(None, "hid", "ep"),
        P(None, "hid", "ep"),
        P(None, "ep", "hid"),
        P("hid", None),
        P(),
        P(),
    )
    out_specs = P("ep", "hid", None, None)
    fits = mesh.shape["hid"] == 4 and mesh.shape["ep"] == 8
    return jax.shard_map(
        pipelined if fits else gathered,
        mesh=mesh,
        in_specs=in_specs,
        out_specs=out_specs,
        check_vma=False,
    )
```

```python
import functools

import jax
import jax.numpy as jnp
from jax import lax
from jax.experimental import pallas as pl
from jax.experimental.pallas import tpu as pltpu
from jax.sharding import PartitionSpec as P

CHUNK_TILES = (1, 1, 2, 2, 2, 2, 2, 1, 1)
MATMUL_VMEM = 36 * 2**20
MOVE_VMEM = 8 * 2**20
COST = pl.CostEstimate(flops=25000000000, bytes_accessed=2**10, transcendentals=0)
ORDER = (
    'S0',
    'K0',
    'S1',
    'S2',
    'K1',
    'K2',
    'A0',
    'S3',
    'A1',
    'I0',
    'K3',
    'I1',
    'M0',
    'A2',
    'S4',
    'M1',
    'I2',
    'K4',
    'O0',
    'A3',
    'M2',
    'I3',
    'O1',
    'A4',
    'P0',
    'I4',
    'M3',
    'P1',
    'L0',
    'S5',
    'O2',
    'L1',
    'K5',
    'S6',
    'M4',
    'K6',
    'A5',
    'O3',
    'P2',
    'I5',
    'A6',
    'L2',
    'S7',
    'M5',
    'I6',
    'O4',
    'K7',
    'P3',
    'A7',
    'M6',
    'L3',
    'S8',
    'I7',
    'O5',
    'K8',
    'P4',
    'M7',
    'A8',
    'L4',
    'O6',
    'I8',
    'P5',
    'M8',
    'O7',
    'L5',
    'O8',
    'P6',
    'P7',
    'L6',
    'P8',
    'L7',
    'L8',
)
MARK = jax.ShapeDtypeStruct((8, 128), jnp.float32)
KINDS = 3
SLOT_TOTAL = 4
ROWS_Z = 4
LINK_CAP = 8
AT_MID, AT_OUT, AT_PARTNER, AT_OWN, TABLE = 0, 8, 16, 20, 32
KEEP, SIDE, FAR_KEEP, FAR_SIDE, MID, OUT, CODES = 0, 2, 4, 6, 8, 16, 24
NEAR_CODES, FAR_CODES, MID_CODES, OUT_CODES = (0, 4), (4, 8), (8, 16), (16, 24)


def route_kernel(here_ref, placement_ref, row_count_ref, table_ref, *, owners, hid_total, block_rows):
    hid, ep = here_ref[0], here_ref[1]
    z, y = ep // 2, ep % 2
    experts = placement_ref.shape[0]
    pieces = [(e, s) for e in range(experts) for s in range(owners)]
    owner = {}
    for e in range(experts):
        start = jnp.int32(0)
        found = [jnp.int32(0)] * owners
        for j in range(owners):
            o = placement_ref[e, j]
            stop = start + row_count_ref[e, o] // block_rows
            for s in range(owners):
                q = s * hid_total + hid
                found[s] = jnp.where((start <= q) & (q < stop), o, found[s])
            start = stop
        for s in range(owners):
            owner[e, s] = found[s]
    upper = z >= 2
    mid_row = (z == 1) | (z == 2)

    def half(row):
        return row >= 2

    zero = jnp.int32(0)
    mid_in, mid_out, out_in, out_out = zero, zero, zero, zero
    for i in range(TABLE):
        table_ref[i] = jnp.int32(-1)
    mine, partner = zero, zero
    for e, s in pieces:
        row, side = s // 2, s % 2
        o = owner[e, s]
        drow = o // 2
        goes_up, goes_down = drow >= 2, drow < 2
        crosses = goes_up if row < 2 else goes_down
        from_here_half = jnp.logical_not(upper) if row < 2 else upper
        leaves_mid = crosses & from_here_half
        enters_mid = crosses & jnp.logical_not(from_here_half)
        to_top = (drow == ROWS_Z - 1) if row < ROWS_Z - 1 else jnp.bool_(False)
        to_bottom = (drow == 0) if row > 0 else jnp.bool_(False)
        on_outer = jnp.where(upper, to_top, to_bottom)
        near_far = z == row
        outer_row = jnp.where(upper, ROWS_Z - 1, 0)
        from_outer = mid_row & (outer_row == row)
        code = jnp.where(
            near_far,
            jnp.where(y == side, KEEP + e, SIDE + e),
            jnp.where(
                from_outer,
                jnp.where(y == side, FAR_KEEP + e, FAR_SIDE + e),
                jnp.where(mid_row, MID + mid_in, OUT + out_in),
            ),
        )

        @pl.when(leaves_mid & mid_row)
        def _(mid_out=mid_out, code=code):
            table_ref[AT_MID + mid_out] = code

        @pl.when(on_outer & mid_row)
        def _(out_in=out_in, code=code):
            table_ref[AT_OUT + out_in] = code

        is_mine = o == ep
        is_partner = (drow == z) & (o != ep)

        @pl.when(is_mine)
        def _(mine=mine, code=code):
            table_ref[AT_OWN + mine] = code

        @pl.when(is_partner)
        def _(partner=partner, code=code):
            table_ref[AT_PARTNER + partner] = code

        mid_out = mid_out + leaves_mid.astype(jnp.int32)
        mid_in = mid_in + enters_mid.astype(jnp.int32)
        out_in = out_in + on_outer.astype(jnp.int32)
        mine = mine + is_mine.astype(jnp.int32)
        partner = partner + is_partner.astype(jnp.int32)


def route(here, placement, row_count, hid_total, block_rows):
    smem = pl.BlockSpec(memory_space=pltpu.SMEM)
    return pl.pallas_call(
        functools.partial(
            route_kernel,
            owners=placement.shape[1],
            hid_total=hid_total,
            block_rows=block_rows,
        ),
        out_shape=jax.ShapeDtypeStruct((TABLE,), jnp.int32),
        in_specs=[smem] * 3,
        out_specs=smem,
        compiler_params=pltpu.CompilerParams(vmem_limit_bytes=MOVE_VMEM),
        name="route",
    )(here, placement, row_count)


ANYWHERE = pl.BlockSpec(memory_space=pl.ANY)
ON_SMEM = pl.BlockSpec(memory_space=pltpu.SMEM)
ON_VMEM = pl.BlockSpec(memory_space=pltpu.VMEM)
ON_HBM = pl.BlockSpec(memory_space=pltpu.HBM)
TILE = 256


def gather_rows_kernel(gate_ref, up_ref, down_ref, out_ref):
    rows = out_ref.shape[4]
    for kind, ref in enumerate((gate_ref, up_ref, down_ref)):
        block = ref[0] if kind == 2 else ref[0].T
        for x in range(2):
            for core in range(2):
                first = (2 * x + core) * rows
                out_ref[core, x, 0, kind] = block[first : first + rows]


def gather_rows(gate_proj, up_proj, down_proj):
    experts, depth, local_rows = gate_proj.shape
    block_rows = local_rows // 4
    across = pl.BlockSpec((1, depth, local_rows), lambda e: (e, 0, 0))
    along = pl.BlockSpec((1, local_rows, depth), lambda e: (e, 0, 0))
    rows = pl.pallas_call(
        gather_rows_kernel,
        out_shape=jax.ShapeDtypeStruct((2, 2, experts, KINDS, block_rows, depth), jnp.bfloat16),
        grid=(experts,),
        in_specs=[across, across, along],
        out_specs=pl.BlockSpec(
            (2, 2, 1, KINDS, block_rows, depth), lambda e: (0, 0, e, 0, 0, 0)
        ),
        compiler_params=pltpu.CompilerParams(vmem_limit_bytes=32 * 2**20),
        name="gather_rows",
    )(gate_proj, up_proj, down_proj)
    return rows.reshape(2, 2 * experts * KINDS * block_rows, depth)


def each_tile(lhs, rot_ref, tile_ref, sems, column, width, use):
    total = width // TILE

    def tile_copy(index):
        slot = lax.rem(index, 2)
        columns = pl.ds(pl.multiple_of(column + index * TILE, TILE), TILE)
        return pltpu.make_async_copy(rot_ref.at[:, columns], tile_ref.at[slot], sems.at[slot])

    tile_copy(0).start()

    @pl.loop(0, total)
    def _(index):
        @pl.when(index + 1 < total)
        def _():
            tile_copy(index + 1).start()

        tile_copy(index).wait()
        result = jnp.dot(
            lhs[...], tile_ref[lax.rem(index, 2)], preferred_element_type=jnp.float32
        )
        use(pl.ds(pl.multiple_of(index * TILE, TILE), TILE), result)


def send_kernel(here_ref, lhs_ref, rot_ref, after_ref, out_ref, mark_ref, *scratch, column):
    def use(columns, result):
        out_ref[:, columns] = result.astype(jnp.bfloat16)

    lhs = lhs_ref.at[1 - here_ref[0] % 2]
    each_tile(lhs, rot_ref, *scratch, column, out_ref.shape[1], use)


def keep_kernel(
    here_ref, lhs_ref, rot_ref, recv_ref, after_ref, away_ref, home_ref, mark_ref, *scratch, column
):
    rows, width = away_ref.shape
    x = here_ref[0] // 2

    def use(columns, result):
        total = (result + recv_ref[:, columns].astype(jnp.float32)).astype(jnp.bfloat16)

        @pl.when(x == 0)
        def _():
            home_ref[:, columns] = total[:rows]
            away_ref[:, columns] = total[rows:]

        @pl.when(x == 1)
        def _():
            home_ref[:, columns] = total[rows:]
            away_ref[:, columns] = total[:rows]

    lhs = lhs_ref.at[here_ref[0] % 2]
    each_tile(lhs, rot_ref, *scratch, column, width, use)


def tile_scratch(depth):
    return [pltpu.VMEM((2, depth, TILE), jnp.bfloat16), pltpu.SemaphoreType.DMA((2,))]


def matmul_send(here, lhs, rotation, column, width, after, cost):
    _, rows, depth = lhs.shape
    return pl.pallas_call(
        functools.partial(send_kernel, column=column),
        out_shape=(jax.ShapeDtypeStruct((rows, width), jnp.bfloat16), MARK),
        in_specs=[ON_SMEM, ON_VMEM, ON_HBM, ANYWHERE],
        out_specs=(ON_VMEM, ANYWHERE),
        scratch_shapes=tile_scratch(depth),
        compiler_params=pltpu.CompilerParams(vmem_limit_bytes=MATMUL_VMEM),
        cost_estimate=cost,
        name="matmul_send",
    )(here, lhs, rotation, after)


def matmul_keep(here, lhs, rotation, recv, column, width, after, cost):
    _, rows, depth = lhs.shape
    out = jax.ShapeDtypeStruct((rows // 2, width), jnp.bfloat16)
    return pl.pallas_call(
        functools.partial(keep_kernel, column=column),
        out_shape=(out, out, MARK),
        in_specs=[ON_SMEM, ON_VMEM, ON_HBM, ON_VMEM, ANYWHERE],
        out_specs=(ON_VMEM, ON_VMEM, ANYWHERE),
        scratch_shapes=tile_scratch(depth),
        compiler_params=pltpu.CompilerParams(vmem_limit_bytes=MATMUL_VMEM),
        cost_estimate=cost,
        name="matmul_keep",
    )(here, lhs, rotation, recv, after)


def add_kernel(here_ref, home_ref, recv_ref, after_ref, side_ref, keep_ref, mark_ref):
    width = side_ref.shape[1]
    y = here_ref[1] % 2
    for half, ref in ((1 - y, side_ref), (y, keep_ref)):
        part = pl.ds(pl.multiple_of(half * width, 128), width)
        total = home_ref[:, part].astype(jnp.float32) + recv_ref[:, part].astype(jnp.float32)
        ref[...] = total.astype(jnp.bfloat16)


def add(here, home, recv, after, cost):
    rows, width = home.shape
    tile = 128
    out = jax.ShapeDtypeStruct((rows, width // 2), jnp.bfloat16)
    in_spec = pl.BlockSpec((tile, width), lambda i, here: (i, 0))
    out_spec = pl.BlockSpec((tile, width // 2), lambda i, here: (i, 0))
    return pl.pallas_call(
        add_kernel,
        out_shape=(out, out, MARK),
        grid_spec=pltpu.PrefetchScalarGridSpec(
            num_scalar_prefetch=1,
            grid=(rows // tile,),
            in_specs=[in_spec, in_spec, ANYWHERE],
            out_specs=(out_spec, out_spec, ANYWHERE),
        ),
        compiler_params=pltpu.CompilerParams(vmem_limit_bytes=MOVE_VMEM),
        cost_estimate=cost,
        name="add",
    )(here, home, recv, after)


def start_pick(code, bases, sources, target, sem):
    for source, (low, high) in zip(sources, bases):

        @pl.when((code >= low) & (code < high))
        def _(source=source, low=low):
            pltpu.make_async_copy(source.at[code - low], target, sem).start()


def pick_kernel(table_ref, *refs, first, bases):
    sources, out_ref, sems = refs[: len(bases)], refs[-3], refs[-1]
    total = out_ref.shape[0]
    for i in range(total):
        start_pick(table_ref[first + i], bases, sources, out_ref.at[i], sems.at[i])
    for i in range(total):

        @pl.when(table_ref[first + i] >= 0)
        def _(i=i):
            pltpu.make_async_copy(sources[0].at[0], out_ref.at[i], sems.at[i]).wait()


def pick(table, sources, bases, first, total, after, cost):
    piece = sources[0].shape[1:]
    return pl.pallas_call(
        functools.partial(pick_kernel, first=first, bases=bases),
        out_shape=(jax.ShapeDtypeStruct((total,) + piece, jnp.bfloat16), MARK),
        in_specs=[ON_SMEM] + [ANYWHERE] * (len(sources) + 1),
        out_specs=(ON_VMEM, ANYWHERE),
        scratch_shapes=[pltpu.SemaphoreType.DMA((total,))],
        cost_estimate=cost,
        compiler_params=pltpu.CompilerParams(vmem_limit_bytes=MOVE_VMEM),
        name="pick",
    )(table, *sources, after)


def pack_kernel(keep_ref, side_ref, after_ref, out_ref, mark_ref, sems):
    experts = keep_ref.shape[0]
    copies = [
        pltpu.make_async_copy(ref, out_ref.at[pl.ds(n * experts, experts)], sems.at[n])
        for n, ref in enumerate((keep_ref, side_ref))
    ]
    for copy in copies:
        copy.start()
    for copy in copies:
        copy.wait()


def pack(keep, side, after, cost):
    experts = keep.shape[0]
    return pl.pallas_call(
        pack_kernel,
        out_shape=(jax.ShapeDtypeStruct((2 * experts,) + keep.shape[1:], jnp.bfloat16), MARK),
        in_specs=[ANYWHERE] * 3,
        out_specs=(ON_VMEM, ANYWHERE),
        scratch_shapes=[pltpu.SemaphoreType.DMA((2,))],
        compiler_params=pltpu.CompilerParams(vmem_limit_bytes=MOVE_VMEM),
        cost_estimate=cost,
        name="pack",
    )(keep, side, after)


def place_kernel(here_ref, table_ref, *refs, bases, column):
    sources, partner_ref = refs[: len(bases)], refs[len(bases)]
    out_ref, mark_ref, held_ref, in_sems, out_sems = refs[-5:]
    _, _, _, rows, width = held_ref.shape
    y = here_ref[1] % 2

    def target(slot, half):
        at = pl.multiple_of(column + half * width, 128)
        return out_ref.at[:, pl.ds(slot * rows, rows), pl.ds(at, width)]

    for slot in range(SLOT_TOTAL):
        code = table_ref[AT_OWN + slot]
        start_pick(code, bases, sources, held_ref.at[slot, 0], in_sems.at[slot, 0])

        @pl.when(code >= 0)
        def _(slot=slot):
            pltpu.make_async_copy(
                partner_ref.at[slot], held_ref.at[slot, 1], in_sems.at[slot, 1]
            ).start()

        @pl.when(code < 0)
        def _(slot=slot):
            held_ref[slot] = jnp.zeros(held_ref.shape[1:], held_ref.dtype)

    for slot in range(SLOT_TOTAL):

        @pl.when(table_ref[AT_OWN + slot] >= 0)
        def _(slot=slot):
            for part in range(2):
                pltpu.make_async_copy(
                    partner_ref.at[slot], held_ref.at[slot, part], in_sems.at[slot, part]
                ).wait()

        pltpu.make_async_copy(held_ref.at[slot, 0], target(slot, y), out_sems.at[slot, 0]).start()
        pltpu.make_async_copy(
            held_ref.at[slot, 1], target(slot, 1 - y), out_sems.at[slot, 1]
        ).start()
    for slot in range(SLOT_TOTAL):
        pltpu.make_async_copy(held_ref.at[slot, 0], target(slot, y), out_sems.at[slot, 0]).wait()
        pltpu.make_async_copy(
            held_ref.at[slot, 1], target(slot, 1 - y), out_sems.at[slot, 1]
        ).wait()


def place(here, table, sources, bases, partner, column, full_width, previous, after, cost):
    piece = partner.shape[1:]
    operands = [here, table, *sources, partner, after]
    in_specs = [ON_SMEM, ON_SMEM] + [ANYWHERE] * (len(sources) + 2)
    aliases = {}
    if previous is not None:
        aliases = {len(operands): 0}
        operands.append(previous)
        in_specs.append(ANYWHERE)
    return pl.pallas_call(
        functools.partial(place_kernel, bases=bases, column=column),
        out_shape=(
            jax.ShapeDtypeStruct((KINDS, SLOT_TOTAL * piece[1], full_width), jnp.bfloat16),
            MARK,
        ),
        in_specs=in_specs,
        out_specs=(ANYWHERE, ANYWHERE),
        scratch_shapes=[
            pltpu.VMEM((SLOT_TOTAL, 2) + piece, jnp.bfloat16),
            pltpu.SemaphoreType.DMA((SLOT_TOTAL, 2)),
            pltpu.SemaphoreType.DMA((SLOT_TOTAL, 2)),
        ],
        input_output_aliases=aliases,
        cost_estimate=cost,
        compiler_params=pltpu.CompilerParams(vmem_limit_bytes=MOVE_VMEM),
        name="place",
    )(*operands)


def pipelined(gate_proj, up_proj, down_proj, rotation, placement, row_count):
    hid_total = lax.axis_size("hid")
    experts, depth, local_rows = gate_proj.shape
    full_width = rotation.shape[1]
    block_rows = local_rows // hid_total
    here = jnp.stack([lax.axis_index("hid"), lax.axis_index("ep")]).astype(jnp.int32)
    table = route(here, placement, row_count, hid_total, block_rows)

    lhs = gather_rows(gate_proj, up_proj, down_proj)

    cores = [(h, h ^ 1) for h in range(4)]
    along_x = [(h, h ^ 2) for h in range(4)]
    along_y = [(s, s ^ 1) for s in range(8)]
    inward = [(0, 2), (1, 3), (6, 4), (7, 5)]
    middle = [(2, 4), (3, 5), (4, 2), (5, 3)]
    outward = [(4, 6), (5, 7), (2, 0), (3, 1)]
    widths = [2 * tiles * TILE for tiles in CHUNK_TILES]
    columns = [sum(widths[:i]) for i in range(len(widths))]
    chunks = len(widths)

    core_recv, x_recv, home, keep, side = {}, {}, {}, {}, {}
    near, far, mid, outer, partner = {}, {}, {}, {}, {}
    all_codes = [NEAR_CODES, FAR_CODES, MID_CODES, OUT_CODES]

    def send_terms(i, served, *order):
        sent, mark = matmul_send(here, lhs, rotation, columns[i], widths[i], *order)
        core_recv[i] = lax.ppermute(sent, "hid", cores)
        return served, mark

    def keep_terms(i, served, *order):
        recv = core_recv.pop(i)
        away, home[i], mark = matmul_keep(here, lhs, rotation, recv, columns[i], widths[i], *order)
        x_recv[i] = lax.ppermute(away, "hid", along_x)
        return served, mark

    def sum_terms(i, served, *order):
        pieces = (experts, KINDS, block_rows, widths[i] // 2)
        out, own, mark = add(here, home.pop(i), x_recv.pop(i), *order)
        keep[i] = own.reshape(pieces)
        side[i] = lax.ppermute(out.reshape(pieces), "ep", along_y)
        return served, mark

    def send_inward(i, served, *order):
        near[i], mark = pack(keep.pop(i), side.pop(i), *order)
        far[i] = lax.ppermute(near[i], "ep", inward)
        return served, mark

    def send_across(i, served, *order):
        codes = [NEAR_CODES, FAR_CODES]
        out, mark = pick(table, [near[i], far[i]], codes, AT_MID, LINK_CAP, *order)
        mid[i] = lax.ppermute(out, "ep", middle)
        return served, mark

    def send_outward(i, served, *order):
        codes = [NEAR_CODES, MID_CODES]
        out, mark = pick(table, [near[i], mid[i]], codes, AT_OUT, LINK_CAP, *order)
        outer[i] = lax.ppermute(out, "ep", outward)
        return served, mark

    def send_partner(i, served, *order):
        sources = [near[i], far[i], mid[i], outer[i]]
        out, mark = pick(table, sources, all_codes, AT_PARTNER, SLOT_TOTAL, *order)
        partner[i] = lax.ppermute(out, "ep", along_y)
        return served, mark

    def put(i, served, *order):
        sources = [near.pop(i), far.pop(i), mid.pop(i), outer.pop(i)]
        return place(
            here, table, sources, all_codes, partner.pop(i), columns[i], full_width, served, *order
        )

    stages = dict(
        S=send_terms,
        K=keep_terms,
        A=sum_terms,
        I=send_inward,
        M=send_across,
        O=send_outward,
        P=send_partner,
        L=put,
    )
    served, mark = None, here
    for step in ORDER:
        served, mark = stages[step[0]](int(step[1:]), served, mark, COST)
    return served.transpose(1, 0, 2)[None]


def count_below(bound, residue, shard_total):
    return (bound + shard_total - 1 - residue) // shard_total


def routing(placement, row_count, block_rows):
    owner_total = placement.shape[1]
    blocks = row_count // block_rows
    onehot = (
        placement[:, :, None] == jnp.arange(owner_total, dtype=jnp.int32)[None, None, :]
    ).astype(jnp.int32)
    ordered = jnp.sum(onehot * blocks[:, None, :], axis=2)
    ordered_start = jnp.cumsum(ordered, axis=1) - ordered
    first_block = jnp.sum(onehot * ordered_start[:, :, None], axis=1)
    return (blocks, first_block)


def assemble(received, received_slot, slot_blocks, experts):
    flat_slot = received_slot.reshape(-1)
    matches = flat_slot[None, :] == jnp.arange(slot_blocks, dtype=jnp.int32)[:, None]
    present = jnp.any(matches, axis=1)
    picked = jnp.argmax(matches, axis=1)
    source_ids = picked // experts
    expert_ids = picked % experts
    chosen = received[source_ids, :, expert_ids]
    chosen = jnp.where(present[:, None, None, None], chosen, jnp.zeros((), jnp.bfloat16))
    return chosen.reshape(1, slot_blocks * chosen.shape[1], chosen.shape[2], chosen.shape[3])


def gathered(gate_proj, up_proj, down_proj, rotation, placement, row_count):
    shard_total = lax.axis_size("hid")
    owner_total = lax.axis_size("ep")
    experts, width_part, local_rows = gate_proj.shape
    full_width = rotation.shape[1]
    block_rows = local_rows // shard_total
    stacked = jnp.stack(
        [
            jnp.transpose(gate_proj, (2, 0, 1)),
            jnp.transpose(up_proj, (2, 0, 1)),
            jnp.transpose(down_proj, (1, 0, 2)),
        ],
        axis=2,
    )
    stacked = stacked.reshape(local_rows, experts * 3, width_part)
    summed = lax.psum_scatter(
        jnp.einsum("fck,kh->fch", stacked, rotation, preferred_element_type=jnp.float32).astype(
            jnp.bfloat16
        ),
        "hid",
        scatter_dimension=0,
        tiled=True,
    )
    rotated = summed.reshape(block_rows, experts, 3, full_width)
    shard_here = lax.axis_index("hid")
    owner_here = lax.axis_index("ep")
    block_here = owner_here * shard_total + shard_here
    blocks, first_block = routing(placement, row_count, block_rows)
    inside = ((first_block <= block_here) & (block_here < first_block + blocks)).astype(jnp.int32)
    owner_ids = jnp.arange(owner_total, dtype=jnp.int32)
    target_owner = jnp.sum(inside * owner_ids[None, :], axis=1)
    at_shard = count_below(first_block + blocks, shard_here, shard_total) - count_below(
        first_block, shard_here, shard_total
    )
    offset = jnp.cumsum(at_shard, axis=0) - at_shard
    slot_index = jnp.sum(
        inside * (offset - count_below(first_block, shard_here, shard_total)), axis=1
    )
    slot_index = slot_index + count_below(block_here, shard_here, shard_total)
    slot_blocks = 2 * experts
    all_blocks, all_owner, all_slot = (
        lax.all_gather(rotated[None], "ep", axis=0, tiled=True),
        lax.all_gather(target_owner[None], "ep", axis=0, tiled=True),
        lax.all_gather(slot_index[None], "ep", axis=0, tiled=True),
    )
    received_slot = jnp.where(all_owner == owner_here, all_slot, -1)
    return assemble(all_blocks, received_slot, slot_blocks, experts)


def solution(mesh):
    in_specs = (
        P(None, "hid", "ep"),
        P(None, "hid", "ep"),
        P(None, "ep", "hid"),
        P("hid", None),
        P(),
        P(),
    )
    out_specs = P("ep", "hid", None, None)
    fits = mesh.shape["hid"] == 4 and mesh.shape["ep"] == 8
    return jax.shard_map(
        pipelined if fits else gathered,
        mesh=mesh,
        in_specs=in_specs,
        out_specs=out_specs,
        check_vma=False,
    )
```
